256 devices in a mesh: bag: 32 (over x, z), head: 8 (over y, core).
Axes of the slice: x: 4, y: 4, z: 8, core: 2. Of those that a mesh axis runs over, the one named last changes fastest.
Arguments:
- latents: bfloat16 [32, 16, 16, 16, 512], P('bag', 'head'), may hold values from -6 to 6
- frame_counts: int32 [32], P('bag'), may hold values from 8 to 16
- routes: int32 [32768, 1], P('bag'), may hold values from 0 to 31; in each aligned block of 128 rows (0 to 127, 128 to 255, ...) at most 6 rows name the same one
- samples: int32 [32768], P('bag'), may hold values from 0 to 3, as said below
- conv_weight: bfloat16 [27, 512, 128], replicated, may hold values from -0.0546875 to 0.0546875
- embed_weight: bfloat16 [512, 2048], replicated, may hold values from -0.25 to 0.25
- qkv_weight: bfloat16 [3, 2048, 2048], P(None, None, 'head')
Outputs:
- attended: bfloat16 [32768, 2048], P(('bag', 'head'))
The draws below stay inside these ranges and needn't reach their ends.
Inputs may be any that keep to these rules, and one draw needn't show every extreme that they name: `routes`: in each aligned block of 128 rows (the tokens of one device) no bag is named by more than 6 rows, a bound that some block reaches. `samples`: all tokens of one clip carry the same sample id, and every id occurs in some clip.
All inputs are finite; a program needn't handle non-finite values.
Results may differ from the reference program's by a relative error of at most 0.013.
Values may be sent and summed in bfloat16 or wider, within the bound.
A program may use at most 128 MiB of HBM per device.

```python
import math
import jax
import jax.numpy as jnp
import numpy as np
from jax import lax

CIN = 512
COUT = 128
HEADS = 32
HDIM = 64
D = 2048
PF = 512
SAMPLES = 4
HT = 16
WT = 16
FRAMES = 16
CLIPS = 32
TOK_DEV = 128
TOKENS = 32768
CAP = 6
SLOTS = 1536
N_BAG = 32


def draw_samples(key, part):
    clip_ids = jax.random.permutation(jax.random.fold_in(key, 11), CLIPS) % SAMPLES
    return jnp.repeat(clip_ids.astype(jnp.int32), TOKENS // CLIPS, total_repeat_length=TOKENS)


def draw_qkv_weight(key, part):
    base = jax.random.normal(key, (3, D, D), jnp.float32) * D ** (-0.5)
    return base.astype(jnp.bfloat16)


def plant(entries, own_key, least, largest):
    spot = [jax.random.randint(jax.random.fold_in(own_key, axis), (), 0, length) for axis, length in enumerate(entries.shape)]
    main_axis = entries.shape.index(max(entries.shape))
    neighbour = spot[:main_axis] + [(spot[main_axis] + 1) % entries.shape[main_axis]] + spot[main_axis + 1:]
    return entries.at[tuple(spot)].set(least).at[tuple(neighbour)].set(largest)


def shard_levels(own_key, dims, split, least, largest):
    factor_of, own = 1.0, jax.random.fold_in(own_key, 6)
    for axis_at, shards_of in split:
        steps = jnp.exp(jax.random.uniform(jax.random.fold_in(own, axis_at), (shards_of,), jnp.float32, least / len(split), largest / len(split)))
        factor_of = factor_of * jnp.repeat(steps, dims[axis_at] // shards_of).reshape([-1 if axis == axis_at else 1 for axis in range(len(dims))])
    return factor_of


def deal_out(own_key, own, number, rows, number_of, top, bound, slope):
    order = jax.random.permutation(own_key, number_of)
    packed, common = portions_of(number_of, rows * top, bound, slope, True), portions_of(number_of, rows * top, bound, slope, False)
    places = jnp.arange(number_of)

    def named(lengths, turn):
        used = int((lengths > 0).sum())
        fixed = max(1, used // 4)
        moved = fixed + (places - fixed + turn * (used - fixed)) % max(1, number_of - fixed)
        return jnp.zeros((number_of,), jnp.int32).at[order[jnp.where(places < fixed, places, moved)]].set(jnp.asarray(lengths, jnp.int32))

    lengths = jnp.where(number % 4 == 0, named(packed, number // 4), named(common, number - number // 4 - 1))
    mixed = jax.random.permutation(jax.random.fold_in(own, 3), number_of)
    donor, taker = mixed[0:number_of // 2 * 2:2], mixed[1:number_of // 2 * 2:2]
    room = jnp.minimum(lengths[donor] - 1, bound - lengths[taker]) // 2
    room = jnp.where((donor == order[0]) | (taker == order[0]) | (lengths[taker] == 0), 0, jnp.maximum(room, 0))
    moved = jax.random.randint(jax.random.fold_in(own, 4), (number_of // 2,), 0, 1 << 20) % (room + 1)
    lengths = lengths.at[donor].add(-moved).at[taker].add(moved)
    items = jnp.searchsorted(jnp.cumsum(lengths), jnp.arange(rows * top), side="right").astype(jnp.int32)
    table = items.reshape(top, rows).T
    table = table[jax.random.permutation(jax.random.fold_in(own, 1), rows)]
    turn = jax.random.randint(jax.random.fold_in(own, 2), (rows, 1), 0, top)
    return jnp.take_along_axis(table, (jnp.arange(top)[None, :] + turn) % top, axis=1)


def portions_of(number_of, total, reach, lean, full):
    portions = [(1 << 20) // math.isqrt(grade ** lean) + 1 for grade in range(1, number_of + 1)]
    largest = reach if full else min(reach, max(-(-total // number_of), total * portions[0] // sum(portions)))
    least = 1 if total - largest >= number_of - 1 else 0
    counts, surplus = [largest] + [least] * (number_of - 1), total - largest - least * (number_of - 1)
    while surplus > 0:
        free = [i for i in range(1, number_of) if counts[i] < largest] or [i for i in range(1, number_of) if counts[i] < reach]
        pool, left = sum([portions[i] for i in free]), surplus
        for i in free:
            extra = min(reach - counts[i], max(1, left * portions[i] // pool), surplus)
            counts[i] = counts[i] + extra
            surplus = surplus - extra
    return np.array(counts)


def bell_draw(own_key, extent, deviation, reach, shards=(), held_as=jnp.bfloat16):
    drawn = jax.random.normal(own_key, extent, jnp.float32) * deviation
    if len(shards) > 0:
        drawn = shard_levels(own_key, extent, shards, -0.22, 0.18) * drawn
    return jnp.clip(drawn, min=-reach, max=reach).astype(held_as)


def setup_inputs(seed: int = 0) -> dict:
    streams_of = jax.random.split(jax.random.key(seed), 8)
    latents = bell_draw(streams_of[0], (CLIPS, FRAMES, HT, WT, CIN), 1.0, 6.0, ((0, 32), (1, 8)))
    frame_counts = plant(jax.random.randint(streams_of[1], (CLIPS,), FRAMES // 2, FRAMES + 1), jax.random.fold_in(streams_of[1], 1), FRAMES // 2, FRAMES).astype(jnp.int32)
    routes_keys = jax.random.split(jax.random.fold_in(streams_of[2], 1), TOKENS // TOK_DEV)
    routes_turns = jax.random.permutation(jax.random.fold_in(streams_of[2], 3), TOKENS // TOK_DEV)
    routes = jax.vmap(lambda own, number: deal_out(jax.random.fold_in(streams_of[2], 2), own, number, TOK_DEV, N_BAG, 1, CAP, 2))(routes_keys, routes_turns).reshape((TOKENS, 1))
    samples = draw_samples(jax.random.fold_in(streams_of[7], 71), 0)
    conv_weight = bell_draw(streams_of[4], (27, CIN, COUT), (27 * CIN) ** -0.5, 0.0546875)
    embed_weight = bell_draw(streams_of[5], (PF, D), PF ** -0.5, 0.25)
    qkv_weight = draw_qkv_weight(jax.random.fold_in(streams_of[7], 71), 0)
    return dict(latents=latents, frame_counts=frame_counts, routes=routes, samples=samples, conv_weight=conv_weight, embed_weight=embed_weight, qkv_weight=qkv_weight)


epsilon = 1e-06
far_below = -1e+30

def patchify(latent_grid):
    frames_in, rows_in, cols_in, chans = latent_grid.shape
    shaped = latent_grid.reshape(frames_in, rows_in // 2, 2, cols_in // 2, 2, chans)
    return shaped.transpose(0, 1, 3, 2, 4, 5).reshape(frames_in * (rows_in // 2) * (cols_in // 2), 4 * chans)

def project(embedded, qkv_weight):
    widened = embedded.astype(jnp.float32)
    normed = (widened * lax.rsqrt(lax.optimization_barrier(jnp.mean(widened * widened, axis=-1, keepdims=True)) + epsilon)).astype(jnp.bfloat16)
    return jnp.einsum('rd,mdc->rmc', normed.astype(jnp.float32), qkv_weight.astype(jnp.float32)).astype(jnp.bfloat16)

def clip_rows(clip_latents, frame_count, conv_weight, embed_weight, qkv_weight):
    frame_live = jnp.arange(FRAMES, dtype=jnp.int32) < frame_count
    masked = clip_latents * frame_live[:, None, None, None].astype(jnp.bfloat16)
    padded = jnp.pad(masked, ((1, 1), (1, 1), (1, 1), (0, 0)))
    accumulated = jnp.zeros((FRAMES * HT * WT, COUT), jnp.float32)
    for offset_t in range(3):
        for offset_h in range(3):
            for offset_w in range(3):
                window = padded[offset_t:offset_t + FRAMES, offset_h:offset_h + HT, offset_w:offset_w + WT]
                accumulated = accumulated + jnp.dot(window.reshape(-1, CIN), conv_weight[9 * offset_t + 3 * offset_h + offset_w], preferred_element_type=jnp.float32)
    latent_grid = (accumulated.reshape(FRAMES, HT, WT, COUT) * frame_live[:, None, None, None].astype(jnp.float32)).astype(jnp.bfloat16)
    patches = patchify(latent_grid)
    embedded = jnp.dot(patches, embed_weight, preferred_element_type=jnp.float32).astype(jnp.bfloat16)
    return project(embedded, qkv_weight)

def bag_attention(rows, slot_labels):
    count_slots = rows.shape[0]
    queries = rows[:, 0].reshape(count_slots, HEADS, HDIM).transpose(1, 0, 2)
    key_rows = rows[:, 1].reshape(count_slots, HEADS, HDIM).transpose(1, 0, 2)
    value_rows = rows[:, 2].reshape(count_slots, HEADS, HDIM).transpose(1, 0, 2)
    admissible = (slot_labels[None, :] == slot_labels[:, None]) & (slot_labels[None, :] >= 0)

    def one_head(operands):
        query_head, key_head, value_head = operands
        scores = jnp.dot(query_head, key_head.T, preferred_element_type=jnp.float32) * HDIM ** (-0.5)
        scores = jnp.where(admissible, scores, far_below)
        shifted = jnp.exp(scores - lax.optimization_barrier(jnp.max(scores, axis=-1, keepdims=True)))
        weights = (shifted / lax.optimization_barrier(jnp.sum(shifted, axis=-1, keepdims=True))).astype(jnp.bfloat16)
        return jnp.dot(weights, value_head, preferred_element_type=jnp.float32).astype(jnp.bfloat16)
    outputs = lax.map(one_head, (queries, key_rows, value_rows))
    return outputs.transpose(1, 0, 2).reshape(count_slots, HEADS * HDIM)

def reference(latents, frame_counts, routes, samples, conv_weight, embed_weight, qkv_weight):

    def per_clip(operands):
        return clip_rows(operands[0], operands[1], conv_weight, embed_weight, qkv_weight)
    qkv = lax.map(per_clip, (latents, frame_counts)).reshape(TOKENS, 3, D)
    per_frame = HT // 2 * (WT // 2)
    per_clip_tokens = FRAMES * per_frame
    token_ids = jnp.arange(TOKENS, dtype=jnp.int32)
    frame_of = token_ids % per_clip_tokens // per_frame
    clip_of = token_ids // per_clip_tokens
    token_live = frame_of < frame_counts[clip_of]
    labels = jnp.where(token_live, samples, -1).astype(jnp.int32)
    route_flat = routes[:, 0]
    blocks = route_flat.reshape(-1, TOK_DEV)
    onehot = (blocks[:, :, None] == jnp.arange(N_BAG, dtype=jnp.int32)[None, None, :]).astype(jnp.int32)
    slot_rank = lax.optimization_barrier(jnp.sum((jnp.cumsum(onehot, axis=1) - onehot) * onehot, axis=2)).reshape(-1)
    position = (token_ids // TOK_DEV * CAP + slot_rank).astype(jnp.int32)
    members = jnp.full((N_BAG, SLOTS), TOKENS, jnp.int32).at[route_flat, position].set(token_ids)

    def one_bag(member_ids):
        filled = member_ids < TOKENS
        safe_ids = jnp.minimum(member_ids, TOKENS - 1)
        slot_labels = jnp.where(filled, labels[safe_ids], -1).astype(jnp.int32)
        return bag_attention(qkv[safe_ids], slot_labels)
    outputs = lax.map(one_bag, members)
    spread = jnp.zeros((TOKENS, D), jnp.bfloat16).at[members.reshape(-1)].set(outputs.reshape(-1, D), mode='drop')
    return jnp.where(token_live[:, None], spread, jnp.zeros((), jnp.bfloat16))
```

```python
import jax
import jax.numpy as jnp
from jax import lax
from jax.experimental import pallas as pl
from jax.experimental.pallas import tpu as pltpu
from jax.sharding import PartitionSpec as P

BAGS = 32
HEAD_DEVS = 8
CORES = 2
TOK = 128
CAP = 6
MSG = 32
ROWS = BAGS * CAP
SLOTS = HEAD_DEVS * ROWS
PER_BAG = HEAD_DEVS * CAP
FRAMES_DEV = 2
CELLS = 256
CIN = 512
COUT = 128
D = 2048
WIDTH = 256
HDIM = 64
QTILE = 128
TILE = 256
SORTED = SLOTS + 64 + TILE
epsilon = 1e-06
far_below = -1e30

MESH = pl.DeviceIdType.MESH
bf16 = jnp.bfloat16
f32 = jnp.float32
i32 = jnp.int32


def iota(shape, dim):
    return lax.broadcasted_iota(i32, shape, dim)


def dot(a, b):
    return jnp.dot(a, b, preferred_element_type=f32)


def greet(bag, head):
    barrier = pltpu.get_barrier_semaphore()

    def along_bag(step, carry):
        pl.semaphore_signal(
            barrier, inc=1, device_id=(lax.rem(bag + step, BAGS), head), device_id_type=MESH
        )
        return carry

    lax.fori_loop(1, BAGS, along_bag, 0)

    def along_head(step, carry):
        pl.semaphore_signal(
            barrier, inc=1, device_id=(bag, lax.rem(head + step, HEAD_DEVS)), device_id_type=MESH
        )
        return carry

    lax.fori_loop(1, HEAD_DEVS, along_head, 0)
    pl.semaphore_wait(barrier, BAGS + HEAD_DEVS - 2)


def front_kernel(
    count_ref,
    routes_ref,
    samples_ref,
    latents_ref,
    conv_ref,
    rows_ref,
    pos_ref,
    plan_ref,
    taps,
    frames,
    sums,
    grid,
    scatter,
    outbox,
    inbox,
    unpack,
    own_rows,
    load_sem,
    tap_sem,
    halo_send,
    halo_recv,
    bag_send,
    bag_recv,
    local_sem,
    head_send,
    head_recv,
):
    bag = lax.axis_index("bag")
    head = lax.axis_index("head")
    core = lax.rem(head, CORES)
    chip = lax.div(head, CORES)
    count = count_ref[0]

    loads = [
        pltpu.make_async_copy(latents_ref.at[f], frames.at[f + 1], load_sem.at[f])
        for f in range(FRAMES_DEV)
    ]
    for load in loads:
        load.start()
    for a in (1, 0, 2):
        for be in range(9):
            pltpu.make_async_copy(
                conv_ref.at[9 * a + be], taps.at[a, :, pl.ds(be * COUT, COUT)], tap_sem.at[a]
            ).start()

    @pl.when(head == 0)
    def _():
        frames[0] = jnp.zeros((CELLS, CIN), bf16)

    @pl.when(head == HEAD_DEVS - 1)
    def _():
        frames[3] = jnp.zeros((CELLS, CIN), bf16)

    greet(bag, head)

    to_right = pltpu.make_async_remote_copy(
        src_ref=latents_ref.at[FRAMES_DEV - 1],
        dst_ref=frames.at[0],
        send_sem=halo_send.at[0],
        recv_sem=halo_recv.at[0],
        device_id=(bag, lax.rem(head + 1, HEAD_DEVS)),
        device_id_type=MESH,
    )
    to_left = pltpu.make_async_remote_copy(
        src_ref=latents_ref.at[0],
        dst_ref=frames.at[3],
        send_sem=halo_send.at[1],
        recv_sem=halo_recv.at[1],
        device_id=(bag, lax.rem(head + HEAD_DEVS - 1, HEAD_DEVS)),
        device_id_type=MESH,
    )

    @pl.when(head < HEAD_DEVS - 1)
    def _():
        to_right.start()

    @pl.when(head > 0)
    def _():
        to_left.start()

    lane = iota((1, TOK), 1)
    bag_row = iota((BAGS, TOK), 0)
    half = (lane >= TOK // 2).astype(i32)
    lanes32 = iota((BAGS, TOK), 1)
    meta = jnp.where(lanes32 == HEAD_DEVS, samples_ref[0:1, 0:1].astype(f32), 0.0)
    for h in range(HEAD_DEVS):
        named = (routes_ref[h : h + 1, :] == bag_row) & (h * FRAMES_DEV + half < count)
        per_bag = jnp.sum(named.astype(f32), axis=1, keepdims=True)
        meta = meta + jnp.where(lanes32 == h, per_bag, 0.0)
    route = routes_ref[pl.ds(head, 1), :]
    live = head * FRAMES_DEV + half < count
    named = ((route == bag_row) & live).astype(f32)
    before = (iota((TOK, TOK), 0) < iota((TOK, TOK), 1)).astype(bf16)
    rank = jnp.sum(named * dot(named.astype(bf16), before), axis=0, keepdims=True)
    target = jnp.where(live, route * MSG + rank.astype(i32), -1000)
    out_row = iota((BAGS * MSG, TOK), 0)
    for q in range(4):
        scatter[:, q * TOK : (q + 1) * TOK] = (out_row == target + CAP * q).astype(f32).astype(bf16)

    sums[...] = jnp.zeros_like(sums)

    def add_taps(slot, a):
        out = slot - a
        frame_id = head * FRAMES_DEV + slot - 1
        scale = jnp.where((frame_id >= 0) & (frame_id < count), 1.0, 0.0)
        cells = (frames[slot].astype(f32) * scale).astype(bf16)
        made = dot(cells, taps[a])
        for e in range(3):
            sums[out, e] += made[:, (3 + e) * COUT : (4 + e) * COUT]
            sums[out, e, 16:CELLS] += made[: CELLS - 16, e * COUT : (e + 1) * COUT]
            sums[out, e, : CELLS - 16] += made[16:, (6 + e) * COUT : (7 + e) * COUT]

    for load in loads:
        load.wait()

    def taps_here(a):
        pltpu.make_async_copy(taps.at[a], taps.at[a], tap_sem.at[a]).wait()

    taps_here(1)
    add_taps(1, 1)
    add_taps(2, 1)
    taps_here(0)
    add_taps(1, 0)
    taps_here(2)
    add_taps(2, 2)

    @pl.when(head > 0)
    def _():
        to_right.wait_recv()

    add_taps(0, 0)

    @pl.when(head < HEAD_DEVS - 1)
    def _():
        to_left.wait_recv()

    add_taps(3, 2)

    column = lax.rem(iota((CELLS, COUT), 0), 16)
    for f in range(FRAMES_DEV):
        scale = jnp.where(head * FRAMES_DEV + f < count, 1.0, 0.0)
        from_left = jnp.where(column == 0, 0.0, pltpu.roll(sums[f, 0], 1, 0))
        from_right = jnp.where(column == 15, 0.0, pltpu.roll(sums[f, 2], CELLS - 1, 0))
        total = (sums[f, 1] + from_left + from_right) * scale
        grid[f * 16 : (f + 1) * 16] = total.reshape(16, 16, COUT)
    quarters = []
    for di in range(2):
        for dj in range(2):
            quarters.extend(grid[2 * r + di, pl.ds(dj, 8, stride=2), :] for r in range(16))
    patches = jnp.concatenate(quarters, axis=0).astype(bf16)

    meta_here = (iota((BAGS * MSG, BAGS), 0) == iota((BAGS * MSG, BAGS), 1) * MSG + 4 * CAP).astype(f32)
    outbox[...] = (dot(scatter[...], patches) + dot(meta_here.astype(bf16), meta.astype(bf16))).astype(bf16)

    def message(ref, at):
        return ref.at[pl.ds(pl.multiple_of(at * MSG, MSG), MSG)]

    own = pltpu.make_async_copy(message(outbox, bag), message(inbox, bag), local_sem.at[0])
    own.start()

    def send(step, carry):
        to = lax.rem(bag + step, BAGS)
        pltpu.make_async_remote_copy(
            src_ref=message(outbox, to),
            dst_ref=message(inbox, bag),
            send_sem=bag_send,
            recv_sem=bag_recv,
            device_id=(to, head),
            device_id_type=MESH,
        ).start()
        return carry

    lax.fori_loop(1, BAGS, send, 0)

    slot = iota((ROWS, BAGS * MSG), 0)
    clip_of = lax.shift_right_logical(slot * 10923, 16)
    wanted = clip_of * MSG + (slot - clip_of * CAP)
    at_col = iota((ROWS, BAGS * MSG), 1)
    for q in range(4):
        unpack[q * ROWS : (q + 1) * ROWS] = (at_col == wanted + q * CAP).astype(f32).astype(bf16)

    own.wait()
    others = inbox.at[pl.ds(0, (BAGS - 1) * MSG)]
    pltpu.make_async_copy(others, others, bag_recv).wait()

    unpacked = dot(unpack[...], inbox[...]).astype(bf16)
    for q in range(4):
        own_rows[:, q * COUT : (q + 1) * COUT] = unpacked[q * ROWS : (q + 1) * ROWS]

    sibling = chip * CORES + 1 - core

    def chunk(of):
        return rows_ref.at[pl.ds(pl.multiple_of(of * ROWS, ROWS), ROWS)]

    def push(source, of, to, sem):
        return pltpu.make_async_remote_copy(
            src_ref=source,
            dst_ref=chunk(of),
            send_sem=head_send.at[sem],
            recv_sem=head_recv.at[of],
            device_id=(bag, to),
            device_id_type=MESH,
        )

    pushes = []
    for step in (2, 1, 3):
        to = lax.rem(chip + step, 4) * CORES + core
        pushes.append(push(own_rows, head, to, step))
    pushes.append(push(own_rows, head, sibling, 0))
    for one in pushes:
        one.start()
    keep = pltpu.make_async_copy(own_rows, chunk(head), local_sem.at[1])
    keep.start()

    pick = (iota((BAGS, BAGS * MSG), 1) == iota((BAGS, BAGS * MSG), 0) * MSG + 4 * CAP).astype(f32)
    told = dot(pick.astype(bf16), inbox[...])
    lane_w = iota((BAGS, COUT), 1)
    counts = jnp.where(lane_w < HEAD_DEVS, told, 0.0)
    clip_total = jnp.sum(counts, axis=1, keepdims=True)
    sample = jnp.sum(jnp.where(lane_w == HEAD_DEVS, told, 0.0), axis=1, keepdims=True)
    row_w = iota((BAGS, COUT), 0)

    def turned(column_of):
        return jnp.sum(jnp.where(row_w == lane_w, column_of, 0.0), axis=0, keepdims=True)

    total_row = turned(clip_total)
    sample_row = turned(sample + 1.0) - 1.0
    same_before = (sample_row == sample) & (lane_w < row_w)
    first = jnp.sum(jnp.where(same_before, total_row, 0.0), axis=1, keepdims=True)
    plan_lane = iota((1, COUT), 1)
    start = jnp.zeros((1, 1), f32)
    by_sample = jnp.zeros((1, COUT), f32)
    for s in range(4):
        first = first + jnp.where(sample == s, start, 0.0)
        size = jnp.sum(jnp.where(sample == s, clip_total, 0.0), axis=0, keepdims=True)
        by_sample = by_sample + jnp.where(plan_lane == s, start, 0.0)
        by_sample = by_sample + jnp.where(plan_lane == 8 + s, size, 0.0)
        start = start + jnp.ceil(size * 0.0625) * 16.0
    plan_row = iota((8, COUT), 0)
    plan = jnp.where(plan_row == 0, turned(first), jnp.where(plan_row == 1, by_sample, 0.0))
    plan_ref[...] = plan.astype(i32)
    slot_of = iota((BAGS, ROWS), 1)
    clip_col = lax.shift_right_logical(slot_of * 10923, 16)
    in_clip = clip_col == iota((BAGS, ROWS), 0)
    slot_row = iota((1, ROWS), 1)
    rank_row = (slot_row - lax.shift_right_logical(slot_row * 10923, 16) * CAP).astype(f32)
    at = first
    for h in range(HEAD_DEVS):
        here = counts[:, h : h + 1]
        at_row = jnp.sum(jnp.where(in_clip, at, 0.0), axis=0, keepdims=True)
        here_row = jnp.sum(jnp.where(in_clip, here, 0.0), axis=0, keepdims=True)
        pos = jnp.where(rank_row < here_row, at_row + rank_row, -1.0)
        pos_ref[h : h + 1, :] = pos.astype(i32)
        at = at + here

    relays = []
    for step in (1, 3, 2):
        of = lax.rem(chip + step, 4) * CORES + core
        pltpu.make_async_copy(chunk(of), chunk(of), head_recv.at[of]).wait()
        relay = push(chunk(of), of, sibling, 3 + step)
        relay.start()
        relays.append(relay)
    for step in range(4):
        of = lax.rem(chip + step, 4) * CORES + 1 - core
        pltpu.make_async_copy(chunk(of), chunk(of), head_recv.at[of]).wait()
    keep.wait()
    for one in pushes + relays:
        one.wait_send()
    sent = outbox.at[pl.ds(0, (BAGS - 1) * MSG)]
    pltpu.make_async_copy(sent, sent, bag_send).wait()

    @pl.when(head < HEAD_DEVS - 1)
    def _():
        to_right.wait_send()

    @pl.when(head > 0)
    def _():
        to_left.wait_send()


def bag_kernel(plan_ref, pos_ref, rows_ref, embed_ref, qkv_ref, out_ref, q_ref, k_ref, v_ref, o_ref):
    v_ref[...] = jnp.zeros_like(v_ref)
    o_ref[...] = jnp.zeros_like(o_ref)
    end = plan_ref[1, 3] + plan_ref[1, 11]

    def project(tile, carry):
        base = pl.multiple_of(tile * TILE, TILE)
        wanted = iota((TILE, ROWS), 0) + base
        picked = jnp.zeros((TILE, CIN), f32)
        for h in range(HEAD_DEVS):
            chosen = (pos_ref[h : h + 1, :] == wanted).astype(f32).astype(bf16)
            picked = picked + dot(chosen, rows_ref[h * ROWS : (h + 1) * ROWS])
        embedded = dot(picked.astype(bf16), embed_ref[...]).astype(bf16).astype(f32)
        scale = lax.rsqrt(jnp.mean(embedded * embedded, axis=-1, keepdims=True) + epsilon)
        normed = (embedded * scale).astype(bf16)
        q_ref[pl.ds(base, TILE)] = (dot(normed, qkv_ref[0]).astype(bf16) * HDIM**-0.5).astype(bf16)
        k_ref[pl.ds(base, TILE)] = dot(normed, qkv_ref[1]).astype(bf16)
        v_ref[pl.ds(base, TILE)] = dot(normed, qkv_ref[2]).astype(bf16)
        return carry

    lax.fori_loop(0, lax.div(end + TILE - 1, TILE), project, 0)

    heads = WIDTH // HDIM
    head_of = lax.shift_right_logical(iota((QTILE, WIDTH), 1), 6)
    key_at = iota((heads * QTILE, TILE), 1)

    for s in range(4):
        start, size = plan_ref[1, s], plan_ref[1, 8 + s]

        def queries(tile, carry, start=start, size=size):
            q0 = pl.multiple_of(start + tile * QTILE, 16)
            block = q_ref[pl.ds(q0, QTILE)].astype(f32)
            spread = jnp.concatenate(
                [jnp.where(head_of == h, block, 0.0) for h in range(heads)], axis=0
            ).astype(bf16)

            def keys(step, state):
                top, norm, total = state
                k0 = pl.multiple_of(start + step * TILE, 16)
                scores = lax.dot_general(
                    spread, k_ref[pl.ds(k0, TILE)], (((1,), (1,)), ((), ())), preferred_element_type=f32
                )
                scores = jnp.where(key_at + step * TILE < size, scores, far_below)
                higher = jnp.maximum(top, jnp.max(scores, axis=-1, keepdims=True))
                shifted = jnp.exp(scores - higher)
                fade = jnp.exp(top - higher)
                norm = norm * fade + jnp.sum(shifted, axis=-1, keepdims=True)
                total = total * fade + dot(shifted.astype(bf16), v_ref[pl.ds(k0, TILE)])
                return higher, norm, total

            state = (
                jnp.full((heads * QTILE, 1), far_below, f32),
                jnp.zeros((heads * QTILE, 1), f32),
                jnp.zeros((heads * QTILE, WIDTH), f32),
            )
            _, norm, total = lax.fori_loop(0, lax.div(size + TILE - 1, TILE), keys, state)
            total = total / norm
            mixed = jnp.zeros((QTILE, WIDTH), f32)
            for h in range(heads):
                mixed = mixed + jnp.where(head_of == h, total[h * QTILE : (h + 1) * QTILE], 0.0)
            o_ref[pl.ds(q0, QTILE)] = mixed
            return carry

        lax.fori_loop(0, lax.div(size + QTILE - 1, QTILE), queries, 0)

    for c in range(BAGS):
        first = plan_ref[0, c]
        over = lax.rem(first, 8)
        block = o_ref[pl.ds(pl.multiple_of(first - over, 8), PER_BAG + 8), :]
        block = pltpu.roll(block, lax.rem(PER_BAG + 8 - over, PER_BAG + 8), 0)
        out_ref[c * PER_BAG : (c + 1) * PER_BAG] = block[:PER_BAG].astype(bf16)


def back_kernel(
    count_ref,
    routes_ref,
    mixed_ref,
    out_ref,
    inbox,
    gather,
    home,
    bag_send,
    bag_recv,
    local_sem,
    head_send,
    head_recv,
):
    bag = lax.axis_index("bag")
    head = lax.axis_index("head")
    count = count_ref[0]
    greet(bag, head)

    def message(ref, at):
        return ref.at[pl.ds(pl.multiple_of(at * PER_BAG, PER_BAG), PER_BAG)]

    own = pltpu.make_async_copy(message(mixed_ref, bag), message(inbox, bag), local_sem.at[0])
    own.start()

    def send(step, carry):
        to = lax.rem(bag + step, BAGS)
        pltpu.make_async_remote_copy(
            src_ref=message(mixed_ref, to),
            dst_ref=message(inbox, bag),
            send_sem=bag_send,
            recv_sem=bag_recv,
            device_id=(to, head),
            device_id_type=MESH,
        ).start()
        return carry

    lax.fori_loop(1, BAGS, send, 0)

    routes_col = jnp.transpose(routes_ref[...])
    half = (iota((TOK, 1), 0) >= TOK // 2).astype(i32)
    before = (iota((TOK, TOK), 1) < iota((TOK, TOK), 0)).astype(bf16)
    at_col = iota((TOK, SLOTS), 1)
    earlier = jnp.zeros((1, TOK), f32)
    for h in range(HEAD_DEVS):
        route = routes_col[:, h : h + 1]
        live = h * FRAMES_DEV + half < count
        named = ((route == iota((TOK, TOK), 1)) & live).astype(f32)
        rank = jnp.sum(named * (dot(before, named.astype(bf16)) + earlier), axis=1, keepdims=True)
        earlier = earlier + jnp.sum(named, axis=0, keepdims=True)
        target = jnp.where(live, route * PER_BAG + rank.astype(i32), -1)
        gather[h * TOK : (h + 1) * TOK] = (at_col == target).astype(f32).astype(bf16)

    own.wait()
    others = inbox.at[pl.ds(0, (BAGS - 1) * PER_BAG)]
    pltpu.make_async_copy(others, others, bag_recv).wait()

    columns = pl.ds(pl.multiple_of(head * WIDTH, WIDTH), WIDTH)

    def deliver(step, carry):
        to = lax.rem(head + step, HEAD_DEVS)
        at = pl.ds(pl.multiple_of(to * TOK, TOK), TOK)
        home[at] = dot(gather[at], inbox[...]).astype(bf16)
        pltpu.make_async_remote_copy(
            src_ref=home.at[at],
            dst_ref=out_ref.at[:, columns],
            send_sem=head_send,
            recv_sem=head_recv,
            device_id=(bag, to),
            device_id_type=MESH,
        ).start()
        return carry

    lax.fori_loop(1, HEAD_DEVS, deliver, 0)
    at = pl.ds(pl.multiple_of(head * TOK, TOK), TOK)
    home[at] = dot(gather[at], inbox[...]).astype(bf16)
    own = pltpu.make_async_copy(home.at[at], out_ref.at[:, columns], local_sem.at[1])
    own.start()
    own.wait()
    arrived = out_ref.at[:, pl.ds(0, (HEAD_DEVS - 1) * WIDTH)]
    pltpu.make_async_copy(arrived, arrived, head_recv).wait()
    left = home.at[pl.ds(0, (HEAD_DEVS - 1) * TOK)]
    pltpu.make_async_copy(left, left, head_send).wait()
    sent = mixed_ref.at[pl.ds(0, (BAGS - 1) * PER_BAG)]
    pltpu.make_async_copy(sent, sent, bag_send).wait()


SMEM = pl.BlockSpec(memory_space=pltpu.SMEM)
VMEM = pl.BlockSpec(memory_space=pltpu.VMEM)
ANY = pl.BlockSpec(memory_space=pl.ANY)


def shards(latents, frame_counts, routes, samples, conv_weight, embed_weight, qkv_weight):
    routes = routes.reshape(HEAD_DEVS, TOK)
    samples = samples.reshape(HEAD_DEVS, TOK)
    latents = latents.reshape(FRAMES_DEV, CELLS, CIN)
    dma, regular = pltpu.SemaphoreType.DMA, pltpu.SemaphoreType.DMA
    rows, pos, plan = pl.pallas_call(
        front_kernel,
        out_shape=(
            jax.ShapeDtypeStruct((SLOTS, CIN), bf16),
            jax.ShapeDtypeStruct((HEAD_DEVS, ROWS), i32),
            jax.ShapeDtypeStruct((8, COUT), i32),
        ),
        in_specs=[SMEM, VMEM, VMEM, ANY, ANY],
        out_specs=(ANY, VMEM, VMEM),
        scratch_shapes=[
            pltpu.VMEM((3, CIN, 9 * COUT), bf16),
            pltpu.VMEM((4, CELLS, CIN), bf16),
            pltpu.VMEM((FRAMES_DEV, 3, CELLS, COUT), f32),
            pltpu.VMEM((FRAMES_DEV * 16, 16, COUT), f32),
            pltpu.VMEM((BAGS * MSG, 4 * TOK), bf16),
            pltpu.VMEM((BAGS * MSG, COUT), bf16),
            pltpu.VMEM((BAGS * MSG, COUT), bf16),
            pltpu.VMEM((4 * ROWS, BAGS * MSG), bf16),
            pltpu.VMEM((ROWS, CIN), bf16),
            dma((FRAMES_DEV,)),
            dma((3,)),
            dma((2,)),
            dma((2,)),
            dma,
            dma,
            dma((2,)),
            dma((7,)),
            dma((HEAD_DEVS,)),
        ],
        compiler_params=pltpu.CompilerParams(
            collective_id=0, has_side_effects=True, vmem_limit_bytes=40 << 20
        ),
        name="front",
    )(frame_counts, routes, samples, latents, conv_weight)
    mixed = pl.pallas_call(
        bag_kernel,
        out_shape=jax.ShapeDtypeStruct((SLOTS, WIDTH), bf16),
        in_specs=[SMEM, VMEM, VMEM, VMEM, VMEM],
        out_specs=VMEM,
        scratch_shapes=[
            pltpu.VMEM((SORTED, WIDTH), bf16),
            pltpu.VMEM((SORTED, WIDTH), bf16),
            pltpu.VMEM((SORTED, WIDTH), bf16),
            pltpu.VMEM((SORTED, WIDTH), f32),
        ],
        compiler_params=pltpu.CompilerParams(vmem_limit_bytes=48 << 20),
        name="bag",
    )(plan, pos, rows, embed_weight, qkv_weight)
    return pl.pallas_call(
        back_kernel,
        out_shape=jax.ShapeDtypeStruct((TOK, D), bf16),
        in_specs=[SMEM, VMEM, ANY],
        out_specs=ANY,
        scratch_shapes=[
            pltpu.VMEM((SLOTS, WIDTH), bf16),
            pltpu.VMEM((HEAD_DEVS * TOK, SLOTS), bf16),
            pltpu.VMEM((HEAD_DEVS * TOK, WIDTH), bf16),
            dma,
            dma,
            dma((2,)),
            dma,
            dma,
        ],
        compiler_params=pltpu.CompilerParams(
            collective_id=1, has_side_effects=True, vmem_limit_bytes=40 << 20
        ),
        name="back",
    )(frame_counts, routes, mixed)


def solution(mesh):
    placed = (
        P("bag", "head", None, None, None),
        P("bag"),
        P("bag", None),
        P("bag"),
        P(),
        P(),
        P(None, None, "head"),
    )
    return jax.shard_map(
        shards, mesh=mesh, in_specs=placed, out_specs=P(("bag", "head"), None), check_vma=False
    )
```

```python
import jax
import jax.numpy as jnp
from jax import lax
from jax.experimental import pallas as pl
from jax.experimental.pallas import tpu as pltpu
from jax.sharding import PartitionSpec as P

BAGS = 32
HEAD_DEVS = 8
CORES = 2
TOK = 128
CAP = 6
MSG = 32
ROWS = BAGS * CAP
SLOTS = HEAD_DEVS * ROWS
PER_BAG = HEAD_DEVS * CAP
FRAMES_DEV = 2
CELLS = 256
CIN = 512
COUT = 128
D = 2048
WIDTH = 256
HDIM = 64
GROUPS = 4
GROUP_CLIPS = BAGS // GROUPS
PIECE = GROUP_CLIPS * CAP
GROUP = HEAD_DEVS * PIECE
ALIGN = 128
QTILE = 384
KTILE = 384
SORTED = SLOTS + 4 * ALIGN + KTILE
epsilon = 1e-06
far_below = -1e30

MESH = pl.DeviceIdType.MESH
bf16 = jnp.bfloat16
f32 = jnp.float32
i32 = jnp.int32


def iota(shape, dim):
    return lax.broadcasted_iota(i32, shape, dim)


def dot(a, b):
    return jnp.dot(a, b, preferred_element_type=f32)


def greet(bag, head):
    barrier = pltpu.get_barrier_semaphore()

    def along_bag(step, carry):
        pl.semaphore_signal(
            barrier, inc=1, device_id=(lax.rem(bag + step, BAGS), head), device_id_type=MESH
        )
        return carry

    lax.fori_loop(1, BAGS, along_bag, 0)

    def along_head(step, carry):
        pl.semaphore_signal(
            barrier, inc=1, device_id=(bag, lax.rem(head + step, HEAD_DEVS)), device_id_type=MESH
        )
        return carry

    lax.fori_loop(1, HEAD_DEVS, along_head, 0)
    pl.semaphore_wait(barrier, BAGS + HEAD_DEVS - 2)


def front_kernel(
    count_ref,
    routes_ref,
    samples_ref,
    latents_ref,
    conv_ref,
    embed_ref,
    qkv_ref,
    q_ref,
    k_ref,
    v_ref,
    plan_ref,
    valid_ref,
    taps,
    frames,
    sums,
    grid,
    scatter,
    outbox,
    inbox,
    unpack,
    rows,
    embed,
    qkv,
    normed,
    load_sem,
    tap_sem,
    halo_send,
    halo_recv,
    bag_send,
    bag_recv,
    local_sem,
    head_send,
    head_recv,
):
    bag = lax.axis_index("bag")
    head = lax.axis_index("head")
    core = lax.rem(head, CORES)
    chip = lax.div(head, CORES)
    count = count_ref[0]

    loads = [
        pltpu.make_async_copy(latents_ref.at[f], frames.at[f + 1], load_sem.at[f])
        for f in range(FRAMES_DEV)
    ]
    for load in loads:
        load.start()
    for a in (1, 0, 2):
        for be in range(9):
            pltpu.make_async_copy(
                conv_ref.at[9 * a + be], taps.at[a, :, pl.ds(be * COUT, COUT)], tap_sem.at[a]
            ).start()

    weights = [
        pltpu.make_async_copy(embed_ref, embed, load_sem.at[2]),
        pltpu.make_async_copy(qkv_ref, qkv, load_sem.at[3]),
    ]
    for load in weights:
        load.start()

    @pl.when(head == 0)
    def _():
        frames[0] = jnp.zeros((CELLS, CIN), bf16)

    @pl.when(head == HEAD_DEVS - 1)
    def _():
        frames[3] = jnp.zeros((CELLS, CIN), bf16)

    greet(bag, head)

    to_right = pltpu.make_async_remote_copy(
        src_ref=latents_ref.at[FRAMES_DEV - 1],
        dst_ref=frames.at[0],
        send_sem=halo_send.at[0],
        recv_sem=halo_recv.at[0],
        device_id=(bag, lax.rem(head + 1, HEAD_DEVS)),
        device_id_type=MESH,
    )
    to_left = pltpu.make_async_remote_copy(
        src_ref=latents_ref.at[0],
        dst_ref=frames.at[3],
        send_sem=halo_send.at[1],
        recv_sem=halo_recv.at[1],
        device_id=(bag, lax.rem(head + HEAD_DEVS - 1, HEAD_DEVS)),
        device_id_type=MESH,
    )

    @pl.when(head < HEAD_DEVS - 1)
    def _():
        to_right.start()

    @pl.when(head > 0)
    def _():
        to_left.start()

    lane = iota((1, TOK), 1)
    bag_row = iota((BAGS, TOK), 0)
    half = (lane >= TOK // 2).astype(i32)
    lanes32 = iota((BAGS, TOK), 1)
    meta = jnp.where(lanes32 == HEAD_DEVS, samples_ref[0:1, 0:1].astype(f32), 0.0)
    for h in range(HEAD_DEVS):
        named = (routes_ref[h : h + 1, :] == bag_row) & (h * FRAMES_DEV + half < count)
        per_bag = jnp.sum(named.astype(f32), axis=1, keepdims=True)
        meta = meta + jnp.where(lanes32 == h, per_bag, 0.0)
    route = routes_ref[pl.ds(head, 1), :]
    live = head * FRAMES_DEV + half < count
    named = ((route == bag_row) & live).astype(f32)
    before = (iota((TOK, TOK), 0) < iota((TOK, TOK), 1)).astype(bf16)
    rank = jnp.sum(named * dot(named.astype(bf16), before), axis=0, keepdims=True)
    target = jnp.where(live, route * MSG + rank.astype(i32), -1000)
    out_row = iota((BAGS * MSG, TOK), 0)
    for q in range(4):
        scatter[:, q * TOK : (q + 1) * TOK] = (out_row == target + CAP * q).astype(f32).astype(bf16)

    sums[...] = jnp.zeros_like(sums)

    def add_taps(slot, a):
        out = slot - a
        frame_id = head * FRAMES_DEV + slot - 1
        scale = jnp.where((frame_id >= 0) & (frame_id < count), 1.0, 0.0)
        cells = (frames[slot].astype(f32) * scale).astype(bf16)
        made = dot(cells, taps[a])
        for e in range(3):
            sums[out, e] += made[:, (3 + e) * COUT : (4 + e) * COUT]
            sums[out, e, 16:CELLS] += made[: CELLS - 16, e * COUT : (e + 1) * COUT]
            sums[out, e, : CELLS - 16] += made[16:, (6 + e) * COUT : (7 + e) * COUT]

    for load in loads:
        load.wait()

    def taps_here(a):
        pltpu.make_async_copy(taps.at[a], taps.at[a], tap_sem.at[a]).wait()

    taps_here(1)
    add_taps(1, 1)
    add_taps(2, 1)
    taps_here(0)
    add_taps(1, 0)
    taps_here(2)
    add_taps(2, 2)

    @pl.when(head > 0)
    def _():
        to_right.wait_recv()

    add_taps(0, 0)

    @pl.when(head < HEAD_DEVS - 1)
    def _():
        to_left.wait_recv()

    add_taps(3, 2)

    column = lax.rem(iota((CELLS, COUT), 0), 16)
    for f in range(FRAMES_DEV):
        scale = jnp.where(head * FRAMES_DEV + f < count, 1.0, 0.0)
        from_left = jnp.where(column == 0, 0.0, pltpu.roll(sums[f, 0], 1, 0))
        from_right = jnp.where(column == 15, 0.0, pltpu.roll(sums[f, 2], CELLS - 1, 0))
        total = (sums[f, 1] + from_left + from_right) * scale
        grid[f * 16 : (f + 1) * 16] = total.reshape(16, 16, COUT)
    quarters = []
    for di in range(2):
        for dj in range(2):
            quarters.extend(grid[2 * r + di, pl.ds(dj, 8, stride=2), :] for r in range(16))
    patches = jnp.concatenate(quarters, axis=0).astype(bf16)

    meta_here = (iota((BAGS * MSG, BAGS), 0) == iota((BAGS * MSG, BAGS), 1) * MSG + 4 * CAP).astype(f32)
    outbox[...] = (dot(scatter[...], patches) + dot(meta_here.astype(bf16), meta.astype(bf16))).astype(bf16)

    def message(ref, at):
        return ref.at[pl.ds(pl.multiple_of(at * MSG, MSG), MSG)]

    own = pltpu.make_async_copy(message(outbox, bag), message(inbox, bag), local_sem.at[0])
    own.start()

    def send(step, carry):
        to = lax.rem(bag + step, BAGS)
        pltpu.make_async_remote_copy(
            src_ref=message(outbox, to),
            dst_ref=message(inbox, bag),
            send_sem=bag_send,
            recv_sem=bag_recv,
            device_id=(to, head),
            device_id_type=MESH,
        ).start()
        return carry

    lax.fori_loop(1, BAGS, send, 0)

    slot = iota((ROWS, BAGS * MSG), 0)
    clip_of = lax.shift_right_logical(slot * 10923, 16)
    wanted = clip_of * MSG + (slot - clip_of * CAP)
    at_col = iota((ROWS, BAGS * MSG), 1)
    for q in range(4):
        unpack[q * ROWS : (q + 1) * ROWS] = (at_col == wanted + q * CAP).astype(f32).astype(bf16)

    own.wait()
    others = inbox.at[pl.ds(0, (BAGS - 1) * MSG)]
    pltpu.make_async_copy(others, others, bag_recv).wait()

    def piece(of, group):
        return rows.at[pl.ds(pl.multiple_of(group * GROUP + of * PIECE, PIECE), PIECE)]

    unpacked = dot(unpack[...], inbox[...]).astype(bf16)
    for g in range(GROUPS):
        at = pl.ds(pl.multiple_of(g * GROUP + head * PIECE, PIECE), PIECE)
        for q in range(4):
            first_row = q * ROWS + g * PIECE
            rows[at, q * COUT : (q + 1) * COUT] = unpacked[first_row : first_row + PIECE]

    sibling = chip * CORES + 1 - core

    def push(of, group, to, sem):
        return pltpu.make_async_remote_copy(
            src_ref=piece(of, group),
            dst_ref=piece(of, group),
            send_sem=head_send.at[sem],
            recv_sem=head_recv.at[group, of],
            device_id=(bag, to),
            device_id_type=MESH,
        )

    for g in range(GROUPS):
        for step in (2, 1, 3):
            push(head, g, lax.rem(chip + step, 4) * CORES + core, step).start()
        push(head, g, sibling, 0).start()

    pick = (iota((BAGS, BAGS * MSG), 1) == iota((BAGS, BAGS * MSG), 0) * MSG + 4 * CAP).astype(f32)
    told = dot(pick.astype(bf16), inbox[...])
    lane_w = iota((BAGS, COUT), 1)
    row_w = iota((BAGS, COUT), 0)
    counts = jnp.where(lane_w < HEAD_DEVS, told, 0.0)
    clip_total = jnp.sum(counts, axis=1, keepdims=True)
    sample = jnp.sum(jnp.where(lane_w == HEAD_DEVS, told, 0.0), axis=1, keepdims=True)
    lower = (iota((COUT, COUT), 0) < iota((COUT, COUT), 1)).astype(f32)
    earlier = dot(counts.astype(bf16), lower.astype(bf16))

    def turned(column_of):
        return jnp.sum(jnp.where(row_w == lane_w, column_of, 0.0), axis=0, keepdims=True)

    sample_row = turned(sample + 1.0) - 1.0
    same_before = (sample_row == sample) & (lane_w < row_w)
    first = jnp.sum(jnp.where(same_before, 1.0 * PER_BAG, 0.0), axis=1, keepdims=True)
    plan_lane = iota((1, COUT), 1)
    start = jnp.zeros((1, 1), f32)
    by_sample = jnp.zeros((1, COUT), f32)
    for s in range(4):
        first = first + jnp.where(sample == s, start, 0.0)
        size = jnp.sum(jnp.where(sample == s, 1.0 * PER_BAG, 0.0), axis=0, keepdims=True)
        by_sample = by_sample + jnp.where(plan_lane == s, start, 0.0)
        by_sample = by_sample + jnp.where(plan_lane == 8 + s, size, 0.0)
        start = start + jnp.ceil(size * (1.0 / ALIGN)) * ALIGN
    plan_row = iota((8, COUT), 0)
    plan = jnp.where(plan_row == 0, turned(first), jnp.where(plan_row == 1, by_sample, 0.0))
    plan_ref[...] = plan.astype(i32)
    key = iota((BAGS, SORTED), 1).astype(f32)
    held = (key >= first) & (key < first + clip_total)
    valid_ref[...] = jnp.sum(held.astype(f32), axis=0, keepdims=True)

    col = iota((8, GROUP), 1)
    col_head = lax.shift_right_logical(col * 1366, 16)
    in_piece = col - col_head * PIECE
    col_clip = lax.shift_right_logical(in_piece * 10923, 16)
    col_slot = (in_piece - col_clip * CAP).astype(f32)
    clip_row = iota((8, GROUP), 0)
    out_at = iota((GROUP, GROUP), 0).astype(f32)
    targets = []
    for g in range(GROUPS):
        group_counts = counts[g * 8 : (g + 1) * 8]
        group_earlier = earlier[g * 8 : (g + 1) * 8]
        number = jnp.zeros((8, GROUP), f32)
        base = jnp.zeros((8, GROUP), f32)
        for h in range(HEAD_DEVS):
            number = jnp.where(col_head == h, group_counts[:, h : h + 1], number)
            base = jnp.where(col_head == h, group_earlier[:, h : h + 1], base)
        place = jnp.where(col_slot < number, clip_row * 1.0 * PER_BAG + base + col_slot + 1.0, 0.0)
        targets.append(jnp.sum(jnp.where(col_clip == clip_row, place, 0.0), axis=0, keepdims=True) - 1.0)

    def relay(g):
        for step in (1, 3, 2):
            of = lax.rem(chip + step, 4) * CORES + core
            pltpu.make_async_copy(piece(of, g), piece(of, g), head_recv.at[g, of]).wait()
            push(of, g, sibling, 3 + step).start()

    for load in weights:
        load.wait()
    relay(0)
    for g in range(GROUPS):
        for step in range(4):
            of = lax.rem(chip + step, 4) * CORES + 1 - core
            pltpu.make_async_copy(piece(of, g), piece(of, g), head_recv.at[g, of]).wait()
        chosen = (out_at == targets[g]).astype(f32).astype(bf16)
        cells = dot(chosen, rows[g * GROUP : (g + 1) * GROUP]).astype(bf16)
        embedded = dot(cells, embed[...]).astype(bf16).astype(f32)
        if g < GROUPS - 1:
            relay(g + 1)
        scale = lax.rsqrt(jnp.mean(embedded * embedded, axis=-1, keepdims=True) + epsilon)
        normed[...] = (embedded * scale).astype(bf16)
        at = pl.ds(g * GROUP, GROUP)
        q_ref[at] = (dot(normed[...], qkv[0]).astype(bf16) * HDIM**-0.5).astype(bf16)
        k_ref[at] = dot(normed[...], qkv[1]).astype(bf16)
        v_ref[at] = dot(normed[...], qkv[2]).astype(bf16)

    own_pieces = rows.at[pl.ds(0, GROUPS * PIECE)]
    for sem in range(7):
        pltpu.make_async_copy(own_pieces, own_pieces, head_send.at[sem]).wait()
    sent = outbox.at[pl.ds(0, (BAGS - 1) * MSG)]
    pltpu.make_async_copy(sent, sent, bag_send).wait()

    @pl.when(head < HEAD_DEVS - 1)
    def _():
        to_right.wait_send()

    @pl.when(head > 0)
    def _():
        to_left.wait_send()


def bag_kernel(plan_ref, valid_ref, q_in, k_in, v_in, out_ref, q_ref, k_ref, v_ref, o_ref, load_sem):
    moves = ((k_in, k_ref, 0), (q_in, q_ref, 1), (v_in, v_ref, 2))

    def load(c, carry):
        here = pl.ds(pl.multiple_of(c * PER_BAG, PER_BAG), PER_BAG)
        there = pl.ds(pl.multiple_of(plan_ref[0, c], 16), PER_BAG)
        for source, target, sem in moves:
            pltpu.make_async_copy(source.at[here], target.at[there], load_sem.at[sem]).start()
        return carry

    for s in range(4):
        past = pl.multiple_of(plan_ref[1, s] + plan_ref[1, 8 + s], 16)
        v_ref[pl.ds(past, KTILE)] = jnp.zeros((KTILE, WIDTH), bf16)
    lax.fori_loop(0, BAGS, load, 0)
    for source, target, sem in moves:
        pltpu.make_async_copy(source, target.at[pl.ds(0, SLOTS)], load_sem.at[sem]).wait()

    heads = WIDTH // HDIM
    head_of = lax.shift_right_logical(iota((QTILE, WIDTH), 1), 6)

    for s in range(4):
        start, size = plan_ref[1, s], plan_ref[1, 8 + s]

        def queries(tile, carry, start=start, size=size):
            q0 = pl.multiple_of(start + tile * QTILE, ALIGN)
            block = q_ref[pl.ds(q0, QTILE)].astype(f32)
            spread = [jnp.where(head_of == h, block, 0.0).astype(bf16) for h in range(heads)]

            def score(step, h):
                k0 = pl.multiple_of(start + step * KTILE, ALIGN)
                scores = lax.dot_general(
                    spread[h], k_ref[pl.ds(k0, KTILE)], (((1,), (1,)), ((), ())), preferred_element_type=f32
                )
                in_sample = iota((1, KTILE), 1) + step * KTILE < size
                allowed = (valid_ref[:, pl.ds(k0, KTILE)] > 0.0) & in_sample
                scores = jnp.where(allowed, scores, far_below)
                return scores, v_ref[pl.ds(k0, KTILE)]

            steps = lax.div(size + KTILE - 1, KTILE)

            def first(h):
                scores, values = score(0, h)
                top = jnp.max(scores, axis=-1, keepdims=True)
                shifted = jnp.exp(scores - top)
                norm = jnp.sum(shifted, axis=-1, keepdims=True)
                return top, norm, dot(shifted.astype(bf16), values)

            def keys(step, states):
                out = []
                for h in range(heads):
                    top, norm, total = states[h]
                    scores, values = score(step, h)
                    higher = jnp.maximum(top, jnp.max(scores, axis=-1, keepdims=True))
                    shifted = jnp.exp(scores - higher)
                    fade = jnp.exp(top - higher)
                    norm = norm * fade + jnp.sum(shifted, axis=-1, keepdims=True)
                    total = total * fade + dot(shifted.astype(bf16), values)
                    out.append((higher, norm, total))
                return tuple(out)

            def finish(states):
                mixed = jnp.zeros((QTILE, WIDTH), f32)
                for h in range(heads):
                    top, norm, total = states[h]
                    mixed = jnp.where(head_of == h, total * (1.0 / norm), mixed)
                o_ref[pl.ds(q0, QTILE)] = mixed.astype(bf16)

            @pl.when(steps == 1)
            def _():
                mixed = jnp.zeros((QTILE, WIDTH), f32)
                for h in range(heads):
                    top, norm, total = first(h)
                    mixed = jnp.where(head_of == h, total * (1.0 / norm), mixed)
                o_ref[pl.ds(q0, QTILE)] = mixed.astype(bf16)

            @pl.when(steps > 1)
            def _():
                finish(lax.fori_loop(1, steps, keys, tuple(first(h) for h in range(heads))))

            return carry

        lax.fori_loop(0, lax.div(size + QTILE - 1, QTILE), queries, 0)

    for c in range(BAGS):
        there = pl.ds(pl.multiple_of(plan_ref[0, c], 16), PER_BAG)
        out_ref[c * PER_BAG : (c + 1) * PER_BAG] = o_ref[there]


def back_kernel(
    count_ref,
    routes_ref,
    mixed_ref,
    out_ref,
    inbox,
    gather,
    home,
    bag_send,
    bag_recv,
    local_sem,
    head_send,
    head_recv,
):
    bag = lax.axis_index("bag")
    head = lax.axis_index("head")
    count = count_ref[0]
    greet(bag, head)

    def message(ref, at):
        return ref.at[pl.ds(pl.multiple_of(at * PER_BAG, PER_BAG), PER_BAG)]

    own = pltpu.make_async_copy(message(mixed_ref, bag), message(inbox, bag), local_sem.at[0])
    own.start()

    def send(step, carry):
        to = lax.rem(bag + step, BAGS)
        pltpu.make_async_remote_copy(
            src_ref=message(mixed_ref, to),
            dst_ref=message(inbox, bag),
            send_sem=bag_send,
            recv_sem=bag_recv,
            device_id=(to, head),
            device_id_type=MESH,
        ).start()
        return carry

    lax.fori_loop(1, BAGS, send, 0)

    routes_col = jnp.transpose(routes_ref[...])
    half = (iota((TOK, 1), 0) >= TOK // 2).astype(i32)
    before = (iota((TOK, TOK), 1) < iota((TOK, TOK), 0)).astype(bf16)
    at_col = iota((TOK, SLOTS), 1)
    earlier = jnp.zeros((1, TOK), f32)
    for h in range(HEAD_DEVS):
        route = routes_col[:, h : h + 1]
        live = h * FRAMES_DEV + half < count
        named = ((route == iota((TOK, TOK), 1)) & live).astype(f32)
        rank = jnp.sum(named * (dot(before, named.astype(bf16)) + earlier), axis=1, keepdims=True)
        earlier = earlier + jnp.sum(named, axis=0, keepdims=True)
        target = jnp.where(live, route * PER_BAG + rank.astype(i32), -1)
        gather[h * TOK : (h + 1) * TOK] = (at_col == target).astype(f32).astype(bf16)

    own.wait()
    others = inbox.at[pl.ds(0, (BAGS - 1) * PER_BAG)]
    pltpu.make_async_copy(others, others, bag_recv).wait()

    columns = pl.ds(pl.multiple_of(head * WIDTH, WIDTH), WIDTH)

    def deliver(step, carry):
        to = lax.rem(head + step, HEAD_DEVS)
        at = pl.ds(pl.multiple_of(to * TOK, TOK), TOK)
        home[at] = dot(gather[at], inbox[...]).astype(bf16)
        pltpu.make_async_remote_copy(
            src_ref=home.at[at],
            dst_ref=out_ref.at[:, columns],
            send_sem=head_send,
            recv_sem=head_recv,
            device_id=(bag, to),
            device_id_type=MESH,
        ).start()
        return carry

    lax.fori_loop(1, HEAD_DEVS, deliver, 0)
    at = pl.ds(pl.multiple_of(head * TOK, TOK), TOK)
    home[at] = dot(gather[at], inbox[...]).astype(bf16)
    own = pltpu.make_async_copy(home.at[at], out_ref.at[:, columns], local_sem.at[1])
    own.start()
    own.wait()
    arrived = out_ref.at[:, pl.ds(0, (HEAD_DEVS - 1) * WIDTH)]
    pltpu.make_async_copy(arrived, arrived, head_recv).wait()
    left = home.at[pl.ds(0, (HEAD_DEVS - 1) * TOK)]
    pltpu.make_async_copy(left, left, head_send).wait()
    sent = mixed_ref.at[pl.ds(0, (BAGS - 1) * PER_BAG)]
    pltpu.make_async_copy(sent, sent, bag_send).wait()


SMEM = pl.BlockSpec(memory_space=pltpu.SMEM)
VMEM = pl.BlockSpec(memory_space=pltpu.VMEM)
ANY = pl.BlockSpec(memory_space=pl.ANY)


def shards(latents, frame_counts, routes, samples, conv_weight, embed_weight, qkv_weight):
    routes = routes.reshape(HEAD_DEVS, TOK)
    samples = samples.reshape(HEAD_DEVS, TOK)
    latents = latents.reshape(FRAMES_DEV, CELLS, CIN)
    dma = pltpu.SemaphoreType.DMA
    slot_array = jax.ShapeDtypeStruct((SLOTS, WIDTH), bf16)
    q, k, v, plan, valid = pl.pallas_call(
        front_kernel,
        out_shape=(
            slot_array,
            slot_array,
            slot_array,
            jax.ShapeDtypeStruct((8, COUT), i32),
            jax.ShapeDtypeStruct((1, SORTED), f32),
        ),
        in_specs=[SMEM, VMEM, VMEM, ANY, ANY, ANY, ANY],
        out_specs=(VMEM,) * 5,
        scratch_shapes=[
            pltpu.VMEM((3, CIN, 9 * COUT), bf16),
            pltpu.VMEM((4, CELLS, CIN), bf16),
            pltpu.VMEM((FRAMES_DEV, 3, CELLS, COUT), f32),
            pltpu.VMEM((FRAMES_DEV * 16, 16, COUT), f32),
            pltpu.VMEM((BAGS * MSG, 4 * TOK), bf16),
            pltpu.VMEM((BAGS * MSG, COUT), bf16),
            pltpu.VMEM((BAGS * MSG, COUT), bf16),
            pltpu.VMEM((4 * ROWS, BAGS * MSG), bf16),
            pltpu.VMEM((SLOTS, CIN), bf16),
            pltpu.VMEM((CIN, D), bf16),
            pltpu.VMEM((3, D, WIDTH), bf16),
            pltpu.VMEM((GROUP, D), bf16),
            dma((4,)),
            dma((3,)),
            dma((2,)),
            dma((2,)),
            dma,
            dma,
            dma((1,)),
            dma((7,)),
            dma((GROUPS, HEAD_DEVS)),
        ],
        compiler_params=pltpu.CompilerParams(
            collective_id=0, has_side_effects=True, vmem_limit_bytes=56 << 20
        ),
        name="front",
    )(frame_counts, routes, samples, latents, conv_weight, embed_weight, qkv_weight)
    mixed = pl.pallas_call(
        bag_kernel,
        out_shape=slot_array,
        in_specs=[SMEM, VMEM, ANY, ANY, ANY],
        out_specs=VMEM,
        scratch_shapes=[
            pltpu.VMEM((SORTED, WIDTH), bf16),
            pltpu.VMEM((SORTED, WIDTH), bf16),
            pltpu.VMEM((SORTED, WIDTH), bf16),
            pltpu.VMEM((SORTED, WIDTH), bf16),
            dma((3,)),
        ],
        compiler_params=pltpu.CompilerParams(vmem_limit_bytes=56 << 20),
        name="bag",
    )(plan, valid, q, k, v)
    return pl.pallas_call(
        back_kernel,
        out_shape=jax.ShapeDtypeStruct((TOK, D), bf16),
        in_specs=[SMEM, VMEM, ANY],
        out_specs=ANY,
        scratch_shapes=[
            pltpu.VMEM((SLOTS, WIDTH), bf16),
            pltpu.VMEM((HEAD_DEVS * TOK, SLOTS), bf16),
            pltpu.VMEM((HEAD_DEVS * TOK, WIDTH), bf16),
            dma,
            dma,
            dma((2,)),
            dma,
            dma,
        ],
        compiler_params=pltpu.CompilerParams(
            collective_id=1, has_side_effects=True, vmem_limit_bytes=56 << 20
        ),
        name="back",
    )(frame_counts, routes, mixed)


def solution(mesh):
    placed = (
        P("bag", "head", None, None, None),
        P("bag"),
        P("bag", None),
        P("bag"),
        P(),
        P(),
        P(None, None, "head"),
    )
    return jax.shard_map(
        shards, mesh=mesh, in_specs=placed, out_specs=P(("bag", "head"), None), check_vma=False
    )
```

```python
import jax
import jax.numpy as jnp
from jax import lax
from jax.experimental import pallas as pl
from jax.experimental.pallas import tpu as pltpu
from jax.sharding import PartitionSpec as P

BAGS = 32
HEAD_DEVS = 8
CORES = 2
TOK = 128
CAP = 6
MSG = 32
ROWS = BAGS * CAP
SLOTS = HEAD_DEVS * ROWS
PER_BAG = HEAD_DEVS * CAP
FRAMES_DEV = 2
CELLS = 256
CIN = 512
COUT = 128
D = 2048
WIDTH = 256
HDIM = 64
GROUPS = 4
GROUP_CLIPS = BAGS // GROUPS
PIECE = GROUP_CLIPS * CAP
GROUP = HEAD_DEVS * PIECE
ALIGN = 128
QTILE = 384
KTILE = 384
SORTED = SLOTS + 4 * ALIGN + KTILE
epsilon = 1e-06
far_below = -1e30

MESH = pl.DeviceIdType.MESH
bf16 = jnp.bfloat16
f32 = jnp.float32
i32 = jnp.int32


def iota(shape, dim):
    return lax.broadcasted_iota(i32, shape, dim)


def dot(a, b):
    return jnp.dot(a, b, preferred_element_type=f32)


def greet(bag, head):
    barrier = pltpu.get_barrier_semaphore()

    def along_bag(step, carry):
        pl.semaphore_signal(
            barrier, inc=1, device_id=(lax.rem(bag + step, BAGS), head), device_id_type=MESH
        )
        return carry

    def along_head(step, carry):
        pl.semaphore_signal(
            barrier, inc=1, device_id=(bag, lax.rem(head + step, HEAD_DEVS)), device_id_type=MESH
        )
        return carry

    lax.fori_loop(1, HEAD_DEVS, along_head, 0)
    lax.fori_loop(1, BAGS, along_bag, 0)


def met():
    pl.semaphore_wait(pltpu.get_barrier_semaphore(), BAGS + HEAD_DEVS - 2)


def front_kernel(
    count_ref,
    routes_ref,
    samples_ref,
    latents_ref,
    conv_ref,
    embed_ref,
    qkv_ref,
    q_out,
    k_out,
    v_out,
    plan_ref,
    valid_ref,
    taps,
    frames,
    sums,
    edge_out,
    edge_in,
    grid,
    scatter,
    outbox,
    inbox,
    unpack,
    rows,
    embed,
    qkv,
    normed,
    targets,
    q_ref,
    k_ref,
    v_ref,
    load_sem,
    tap_sem,
    halo_send,
    halo_recv,
    bag_send,
    bag_recv,
    local_sem,
    head_send,
    head_recv,
    store_sem,
):
    bag = lax.axis_index("bag")
    head = lax.axis_index("head")
    core = lax.rem(head, CORES)
    chip = lax.div(head, CORES)
    count = count_ref[0]

    loads = [
        pltpu.make_async_copy(latents_ref.at[f], frames.at[f], load_sem.at[f])
        for f in range(FRAMES_DEV)
    ]
    for load in loads:
        load.start()
    for a in (2, 0, 1):
        for be in range(9):
            pltpu.make_async_copy(
                conv_ref.at[9 * a + be], taps.at[a, :, pl.ds(be * COUT, COUT)], tap_sem.at[a]
            ).start()

    weights = [
        pltpu.make_async_copy(embed_ref, embed, load_sem.at[2]),
        pltpu.make_async_copy(qkv_ref, qkv, load_sem.at[3]),
    ]
    for load in weights:
        load.start()

    edge_in[...] = jnp.zeros_like(edge_in)
    greet(bag, head)

    def taps_here(a):
        pltpu.make_async_copy(taps.at[a], taps.at[a], tap_sem.at[a]).wait()

    def add_taps(slot, a, out):
        scale = jnp.where(head * FRAMES_DEV + slot < count, 1.0, 0.0)
        cells = (frames[slot].astype(f32) * scale).astype(bf16)
        made = dot(cells, taps[a])
        for e in range(3):
            sums[out, e] += made[:, (3 + e) * COUT : (4 + e) * COUT]
            sums[out, e, 16:CELLS] += made[: CELLS - 16, e * COUT : (e + 1) * COUT]
            sums[out, e, : CELLS - 16] += made[16:, (6 + e) * COUT : (7 + e) * COUT]

    column = lax.rem(iota((CELLS, COUT), 0), 16)

    def joined(out):
        from_left = jnp.where(column == 0, 0.0, pltpu.roll(sums[out, 0], 1, 0))
        from_right = jnp.where(column == 15, 0.0, pltpu.roll(sums[out, 2], CELLS - 1, 0))
        return sums[out, 1] + from_left + from_right

    sums[...] = jnp.zeros_like(sums)
    loads[0].wait()
    taps_here(2)
    add_taps(0, 2, 2)
    edge_out[1] = joined(2).astype(bf16)
    loads[1].wait()
    taps_here(0)
    add_taps(1, 0, 3)
    edge_out[0] = joined(3).astype(bf16)
    met()

    def edge(side, to):
        return pltpu.make_async_remote_copy(
            src_ref=edge_out.at[side],
            dst_ref=edge_in.at[side],
            send_sem=halo_send.at[side],
            recv_sem=halo_recv.at[side],
            device_id=(bag, to),
            device_id_type=MESH,
        )

    to_right = edge(0, lax.rem(head + 1, HEAD_DEVS))
    to_left = edge(1, lax.rem(head + HEAD_DEVS - 1, HEAD_DEVS))

    @pl.when(head < HEAD_DEVS - 1)
    def _():
        to_right.start()

    @pl.when(head > 0)
    def _():
        to_left.start()

    lane = iota((1, TOK), 1)
    bag_row = iota((BAGS, TOK), 0)
    half = (lane >= TOK // 2).astype(i32)
    lanes32 = iota((BAGS, TOK), 1)
    meta = jnp.where(lanes32 == HEAD_DEVS, samples_ref[0:1, 0:1].astype(f32), 0.0)
    for h in range(HEAD_DEVS):
        named = (routes_ref[h : h + 1, :] == bag_row) & (h * FRAMES_DEV + half < count)
        per_bag = jnp.sum(named.astype(f32), axis=1, keepdims=True)
        meta = meta + jnp.where(lanes32 == h, per_bag, 0.0)
    route = routes_ref[pl.ds(head, 1), :]
    live = head * FRAMES_DEV + half < count
    named = ((route == bag_row) & live).astype(f32)
    before = (iota((TOK, TOK), 0) < iota((TOK, TOK), 1)).astype(bf16)
    rank = jnp.sum(named * dot(named.astype(bf16), before), axis=0, keepdims=True)
    target = jnp.where(live, route * MSG + rank.astype(i32), -1000)
    out_row = iota((BAGS * MSG, TOK), 0)
    for q in range(4):
        scatter[:, q * TOK : (q + 1) * TOK] = (out_row == target + CAP * q).astype(f32).astype(bf16)

    add_taps(0, 0, 1)
    add_taps(1, 2, 0)
    taps_here(1)
    add_taps(0, 1, 0)
    add_taps(1, 1, 1)

    @pl.when(head > 0)
    def _():
        to_right.wait_recv()

    @pl.when(head < HEAD_DEVS - 1)
    def _():
        to_left.wait_recv()

    for f in range(FRAMES_DEV):
        scale = jnp.where(head * FRAMES_DEV + f < count, 1.0, 0.0)
        total = (joined(f) + edge_in[f].astype(f32)) * scale
        grid[f * 16 : (f + 1) * 16] = total.reshape(16, 16, COUT)
    quarters = []
    for di in range(2):
        for dj in range(2):
            quarters.extend(grid[2 * r + di, pl.ds(dj, 8, stride=2), :] for r in range(16))
    patches = jnp.concatenate(quarters, axis=0).astype(bf16)

    meta_here = (iota((BAGS * MSG, BAGS), 0) == iota((BAGS * MSG, BAGS), 1) * MSG + 4 * CAP).astype(f32)
    outbox[...] = (dot(scatter[...], patches) + dot(meta_here.astype(bf16), meta.astype(bf16))).astype(bf16)

    def message(ref, at):
        return ref.at[pl.ds(pl.multiple_of(at * MSG, MSG), MSG)]

    own = pltpu.make_async_copy(message(outbox, bag), message(inbox, bag), local_sem.at[0])
    own.start()

    def send(step, carry):
        to = lax.rem(bag + step, BAGS)
        pltpu.make_async_remote_copy(
            src_ref=message(outbox, to),
            dst_ref=message(inbox, bag),
            send_sem=bag_send,
            recv_sem=bag_recv,
            device_id=(to, head),
            device_id_type=MESH,
        ).start()
        return carry

    lax.fori_loop(1, BAGS, send, 0)

    slot = iota((ROWS, BAGS * MSG), 0)
    clip_of = lax.shift_right_logical(slot * 10923, 16)
    wanted = clip_of * MSG + (slot - clip_of * CAP)
    at_col = iota((ROWS, BAGS * MSG), 1)
    for q in range(4):
        unpack[q * ROWS : (q + 1) * ROWS] = (at_col == wanted + q * CAP).astype(f32).astype(bf16)

    own.wait()
    others = inbox.at[pl.ds(0, (BAGS - 1) * MSG)]
    pltpu.make_async_copy(others, others, bag_recv).wait()

    def piece(of, group):
        return rows.at[pl.ds(pl.multiple_of(group * GROUP + of * PIECE, PIECE), PIECE)]

    unpacked = dot(unpack[...], inbox[...]).astype(bf16)
    for g in range(GROUPS):
        at = pl.ds(pl.multiple_of(g * GROUP + head * PIECE, PIECE), PIECE)
        for q in range(4):
            first_row = q * ROWS + g * PIECE
            rows[at, q * COUT : (q + 1) * COUT] = unpacked[first_row : first_row + PIECE]

    sibling = chip * CORES + 1 - core

    def push(of, group, to, sem):
        return pltpu.make_async_remote_copy(
            src_ref=piece(of, group),
            dst_ref=piece(of, group),
            send_sem=head_send.at[sem],
            recv_sem=head_recv.at[group, of],
            device_id=(bag, to),
            device_id_type=MESH,
        )

    def peer(step):
        return lax.rem(chip + step, 4) * CORES + core

    for g in range(GROUPS):
        push(head, g, peer(1), 1).start()
        push(head, g, peer(3), 3).start()
        push(head, g, sibling, 0).start()

    pick = (iota((BAGS, BAGS * MSG), 1) == iota((BAGS, BAGS * MSG), 0) * MSG + 4 * CAP).astype(f32)
    told = dot(pick.astype(bf16), inbox[...])
    lane_w = iota((BAGS, COUT), 1)
    row_w = iota((BAGS, COUT), 0)
    counts = jnp.where(lane_w < HEAD_DEVS, told, 0.0)
    clip_total = jnp.sum(counts, axis=1, keepdims=True)
    sample = jnp.sum(jnp.where(lane_w == HEAD_DEVS, told, 0.0), axis=1, keepdims=True)
    lower = (iota((COUT, COUT), 0) < iota((COUT, COUT), 1)).astype(f32)
    earlier = dot(counts.astype(bf16), lower.astype(bf16))

    def turned(column_of):
        return jnp.sum(jnp.where(row_w == lane_w, column_of, 0.0), axis=0, keepdims=True)

    sample_row = turned(sample + 1.0) - 1.0
    same_before = (sample_row == sample) & (lane_w < row_w)
    first = jnp.sum(jnp.where(same_before, 1.0 * PER_BAG, 0.0), axis=1, keepdims=True)
    plan_lane = iota((1, COUT), 1)
    start = jnp.zeros((1, 1), f32)
    by_sample = jnp.zeros((1, COUT), f32)
    for s in range(4):
        first = first + jnp.where(sample == s, start, 0.0)
        size = jnp.sum(jnp.where(sample == s, 1.0 * PER_BAG, 0.0), axis=0, keepdims=True)
        by_sample = by_sample + jnp.where(plan_lane == s, start, 0.0)
        by_sample = by_sample + jnp.where(plan_lane == 8 + s, size, 0.0)
        start = start + jnp.ceil(size * (1.0 / ALIGN)) * ALIGN
    plan_row = iota((8, COUT), 0)
    plan = jnp.where(plan_row == 0, turned(first), jnp.where(plan_row == 1, by_sample, 0.0))
    plan_ref[...] = plan.astype(i32)
    key = iota((BAGS, SORTED), 1).astype(f32)
    held = (key >= first) & (key < first + clip_total)
    valid_ref[...] = jnp.sum(held.astype(f32), axis=0, keepdims=True)

    col = iota((8, GROUP), 1)
    col_head = lax.shift_right_logical(col * 1366, 16)
    in_piece = col - col_head * PIECE
    col_clip = lax.shift_right_logical(in_piece * 10923, 16)
    col_slot = (in_piece - col_clip * CAP).astype(f32)
    clip_row = iota((8, GROUP), 0)
    out_at = iota((GROUP, GROUP), 0).astype(f32)
    for g in range(GROUPS):
        group_counts = counts[g * 8 : (g + 1) * 8]
        group_earlier = earlier[g * 8 : (g + 1) * 8]
        number = jnp.zeros((8, GROUP), f32)
        base = jnp.zeros((8, GROUP), f32)
        for h in range(HEAD_DEVS):
            number = jnp.where(col_head == h, group_counts[:, h : h + 1], number)
            base = jnp.where(col_head == h, group_earlier[:, h : h + 1], base)
        place = jnp.where(col_slot < number, clip_row * 1.0 * PER_BAG + base + col_slot + 1.0, 0.0)
        target = jnp.sum(jnp.where(col_clip == clip_row, place, 0.0), axis=0, keepdims=True) - 1.0
        targets[g * 8 : g * 8 + 8] = jnp.broadcast_to(target, (8, GROUP))

    def arrived(of, g):
        pltpu.make_async_copy(piece(of, g), piece(of, g), head_recv.at[g, of]).wait()

    def relay_near(g):
        arrived(peer(1), g)
        arrived(peer(3), g)
        push(peer(3 - 2 * core), g, peer(1 + 2 * core), 2).start()
        push(peer(1), g, sibling, 4).start()
        push(peer(3), g, sibling, 5).start()

    def relay_far(g):
        arrived(peer(2), g)
        push(peer(2), g, sibling, 6).start()

    for load in weights:
        load.wait()
    relay_near(0)
    relay_near(1)
    relay_far(0)

    def stores(g):
        at = pl.ds(pl.multiple_of(g * GROUP, GROUP), GROUP)
        return [
            pltpu.make_async_copy(made.at[at], out.at[at], store_sem.at[m])
            for m, (made, out) in enumerate(((q_ref, q_out), (k_ref, k_out), (v_ref, v_out)))
        ]

    def project(g, carry):
        for step in range(4):
            arrived(lax.rem(chip + step, 4) * CORES + 1 - core, g)
        at = pl.ds(pl.multiple_of(g * GROUP, GROUP), GROUP)
        target = targets[pl.ds(pl.multiple_of(g * 8, 8), 8)][0:1]
        chosen = (out_at == target).astype(f32).astype(bf16)
        cells = dot(chosen, rows[at]).astype(bf16)
        embedded = dot(cells, embed[...]).astype(bf16).astype(f32)

        @pl.when(g < GROUPS - 2)
        def _():
            relay_near(g + 2)

        @pl.when(g < GROUPS - 1)
        def _():
            relay_far(g + 1)

        scale = lax.rsqrt(jnp.mean(embedded * embedded, axis=-1, keepdims=True) + epsilon)
        normed[...] = (embedded * scale).astype(bf16)
        q_ref[at] = (dot(normed[...], qkv[0]).astype(bf16) * HDIM**-0.5).astype(bf16)
        k_ref[at] = dot(normed[...], qkv[1]).astype(bf16)
        v_ref[at] = dot(normed[...], qkv[2]).astype(bf16)
        for store in stores(g):
            store.start()
        return carry

    lax.fori_loop(0, GROUPS, project, 0)

    own_pieces = rows.at[pl.ds(0, GROUPS * PIECE)]
    for sem in range(7):
        pltpu.make_async_copy(own_pieces, own_pieces, head_send.at[sem]).wait()
    for m, (made, out) in enumerate(((q_ref, q_out), (k_ref, k_out), (v_ref, v_out))):
        pltpu.make_async_copy(made, out, store_sem.at[m]).wait()
    sent = outbox.at[pl.ds(0, (BAGS - 1) * MSG)]
    pltpu.make_async_copy(sent, sent, bag_send).wait()

    @pl.when(head < HEAD_DEVS - 1)
    def _():
        to_right.wait_send()

    @pl.when(head > 0)
    def _():
        to_left.wait_send()


def bag_kernel(plan_ref, valid_ref, q_in, k_in, v_in, out_ref, q_ref, k_ref, v_ref, o_ref, load_sem):
    moves = ((k_in, k_ref, 0), (q_in, q_ref, 1), (v_in, v_ref, 2))

    def load(c, carry):
        here = pl.ds(pl.multiple_of(c * PER_BAG, PER_BAG), PER_BAG)
        there = pl.ds(pl.multiple_of(plan_ref[0, c], 16), PER_BAG)
        for source, target, sem in moves:
            pltpu.make_async_copy(source.at[here], target.at[there], load_sem.at[sem]).start()
        return carry

    for s in range(4):
        past = pl.multiple_of(plan_ref[1, s] + plan_ref[1, 8 + s], 16)
        v_ref[pl.ds(past, KTILE)] = jnp.zeros((KTILE, WIDTH), bf16)
    lax.fori_loop(0, BAGS, load, 0)
    for source, target, sem in moves:
        pltpu.make_async_copy(source, target.at[pl.ds(0, SLOTS)], load_sem.at[sem]).wait()

    heads = WIDTH // HDIM
    head_of = lax.shift_right_logical(iota((QTILE, WIDTH), 1), 6)

    def one_sample(s, sample_carry):
        start, size = plan_ref[1, s], plan_ref[1, 8 + s]

        def queries(tile, carry):
            q0 = pl.multiple_of(start + tile * QTILE, ALIGN)
            block = q_ref[pl.ds(q0, QTILE)].astype(f32)
            spread = [jnp.where(head_of == h, block, 0.0).astype(bf16) for h in range(heads)]

            def score(step, h):
                k0 = pl.multiple_of(start + step * KTILE, ALIGN)
                scores = lax.dot_general(
                    spread[h], k_ref[pl.ds(k0, KTILE)], (((1,), (1,)), ((), ())), preferred_element_type=f32
                )
                in_sample = iota((1, KTILE), 1) + step * KTILE < size
                allowed = (valid_ref[:, pl.ds(k0, KTILE)] > 0.0) & in_sample
                scores = jnp.where(allowed, scores, far_below)
                return scores, v_ref[pl.ds(k0, KTILE)]

            steps = lax.div(size + KTILE - 1, KTILE)

            def first(h):
                scores, values = score(0, h)
                top = jnp.max(scores, axis=-1, keepdims=True)
                shifted = jnp.exp(scores - top)
                norm = jnp.sum(shifted, axis=-1, keepdims=True)
                return top, norm, dot(shifted.astype(bf16), values)

            def keys(step, states):
                out = []
                for h in range(heads):
                    top, norm, total = states[h]
                    scores, values = score(step, h)
                    higher = jnp.maximum(top, jnp.max(scores, axis=-1, keepdims=True))
                    shifted = jnp.exp(scores - higher)
                    fade = jnp.exp(top - higher)
                    norm = norm * fade + jnp.sum(shifted, axis=-1, keepdims=True)
                    total = total * fade + dot(shifted.astype(bf16), values)
                    out.append((higher, norm, total))
                return tuple(out)

            def finish(states):
                mixed = jnp.zeros((QTILE, WIDTH), f32)
                for h in range(heads):
                    top, norm, total = states[h]
                    mixed = jnp.where(head_of == h, total * (1.0 / norm), mixed)
                o_ref[pl.ds(q0, QTILE)] = mixed.astype(bf16)

            @pl.when(steps == 1)
            def _():
                mixed = jnp.zeros((QTILE, WIDTH), f32)
                for h in range(heads):
                    top, norm, total = first(h)
                    mixed = jnp.where(head_of == h, total * (1.0 / norm), mixed)
                o_ref[pl.ds(q0, QTILE)] = mixed.astype(bf16)

            @pl.when(steps > 1)
            def _():
                finish(lax.fori_loop(1, steps, keys, tuple(first(h) for h in range(heads))))

            return carry

        lax.fori_loop(0, lax.div(size + QTILE - 1, QTILE), queries, 0)
        return sample_carry

    lax.fori_loop(0, 4, one_sample, 0)

    for c in range(BAGS):
        there = pl.ds(pl.multiple_of(plan_ref[0, c], 16), PER_BAG)
        for half in range(2):
            out_ref[half, c * PER_BAG : (c + 1) * PER_BAG] = o_ref[there, half * COUT : (half + 1) * COUT]


def back_kernel(
    count_ref,
    routes_ref,
    mixed_ref,
    out_ref,
    inbox,
    gather,
    home,
    bag_send,
    bag_recv,
    local_sem,
    head_send,
    head_recv,
):
    bag = lax.axis_index("bag")
    head = lax.axis_index("head")
    count = count_ref[0]
    greet(bag, head)
    met()

    def message(ref, half, at):
        return ref.at[half, pl.ds(pl.multiple_of(at * PER_BAG, PER_BAG), PER_BAG)]

    owns = []
    for half in range(2):

        def send(step, carry, half=half):
            to = lax.rem(bag + step, BAGS)
            pltpu.make_async_remote_copy(
                src_ref=message(mixed_ref, half, to),
                dst_ref=message(inbox, half, bag),
                send_sem=bag_send.at[half],
                recv_sem=bag_recv.at[half],
                device_id=(to, head),
                device_id_type=MESH,
            ).start()
            return carry

        lax.fori_loop(1, BAGS, send, 0)
        own = pltpu.make_async_copy(message(mixed_ref, half, bag), message(inbox, half, bag), local_sem.at[half])
        own.start()
        owns.append(own)

    routes_col = jnp.transpose(routes_ref[...])
    half = (iota((TOK, 1), 0) >= TOK // 2).astype(i32)
    before = (iota((TOK, TOK), 1) < iota((TOK, TOK), 0)).astype(bf16)
    at_col = iota((TOK, SLOTS), 1)
    earlier = jnp.zeros((1, TOK), f32)
    for h in range(HEAD_DEVS):
        route = routes_col[:, h : h + 1]
        live = h * FRAMES_DEV + half < count
        named = ((route == iota((TOK, TOK), 1)) & live).astype(f32)
        rank = jnp.sum(named * (dot(before, named.astype(bf16)) + earlier), axis=1, keepdims=True)
        earlier = earlier + jnp.sum(named, axis=0, keepdims=True)
        target = jnp.where(live, route * PER_BAG + rank.astype(i32), -1)
        gather[h * TOK : (h + 1) * TOK] = (at_col == target).astype(f32).astype(bf16)

    def rest(ref, half):
        return ref.at[half, pl.ds(0, (BAGS - 1) * PER_BAG)]

    def columns(half):
        return pl.ds(pl.multiple_of(head * WIDTH + half * COUT, COUT), COUT)

    keeps = []
    for half in range(2):
        owns[half].wait()
        pltpu.make_async_copy(rest(inbox, half), rest(inbox, half), bag_recv.at[half]).wait()

        def deliver(step, carry, half=half):
            to = lax.rem(head + step, HEAD_DEVS)
            at = pl.ds(pl.multiple_of(to * TOK, TOK), TOK)
            home[half, at] = dot(gather[at], inbox[half]).astype(bf16)
            pltpu.make_async_remote_copy(
                src_ref=home.at[half, at],
                dst_ref=out_ref.at[:, columns(half)],
                send_sem=head_send.at[half],
                recv_sem=head_recv.at[half],
                device_id=(bag, to),
                device_id_type=MESH,
            ).start()
            return carry

        lax.fori_loop(1, HEAD_DEVS, deliver, 0)
        at = pl.ds(pl.multiple_of(head * TOK, TOK), TOK)
        home[half, at] = dot(gather[at], inbox[half]).astype(bf16)
        keep = pltpu.make_async_copy(home.at[half, at], out_ref.at[:, columns(half)], local_sem.at[2 + half])
        keep.start()
        keeps.append(keep)
    for half in range(2):
        keeps[half].wait()
        arrived = out_ref.at[:, pl.ds(0, (HEAD_DEVS - 1) * COUT)]
        pltpu.make_async_copy(arrived, arrived, head_recv.at[half]).wait()
        left = home.at[half, pl.ds(0, (HEAD_DEVS - 1) * TOK)]
        pltpu.make_async_copy(left, left, head_send.at[half]).wait()
        pltpu.make_async_copy(rest(mixed_ref, half), rest(mixed_ref, half), bag_send.at[half]).wait()


SMEM = pl.BlockSpec(memory_space=pltpu.SMEM)
VMEM = pl.BlockSpec(memory_space=pltpu.VMEM)
ANY = pl.BlockSpec(memory_space=pl.ANY)


def shards(latents, frame_counts, routes, samples, conv_weight, embed_weight, qkv_weight):
    routes = routes.reshape(HEAD_DEVS, TOK)
    samples = samples.reshape(HEAD_DEVS, TOK)
    latents = latents.reshape(FRAMES_DEV, CELLS, CIN)
    dma = pltpu.SemaphoreType.DMA
    slot_array = jax.ShapeDtypeStruct((SLOTS, WIDTH), bf16)
    q, k, v, plan, valid = pl.pallas_call(
        front_kernel,
        out_shape=(
            slot_array,
            slot_array,
            slot_array,
            jax.ShapeDtypeStruct((8, COUT), i32),
            jax.ShapeDtypeStruct((1, SORTED), f32),
        ),
        in_specs=[SMEM, VMEM, VMEM, ANY, ANY, ANY, ANY],
        out_specs=(ANY, ANY, ANY, VMEM, VMEM),
        scratch_shapes=[
            pltpu.VMEM((3, CIN, 9 * COUT), bf16),
            pltpu.VMEM((FRAMES_DEV, CELLS, CIN), bf16),
            pltpu.VMEM((FRAMES_DEV + 2, 3, CELLS, COUT), f32),
            pltpu.VMEM((2, CELLS, COUT), bf16),
            pltpu.VMEM((2, CELLS, COUT), bf16),
            pltpu.VMEM((FRAMES_DEV * 16, 16, COUT), f32),
            pltpu.VMEM((BAGS * MSG, 4 * TOK), bf16),
            pltpu.VMEM((BAGS * MSG, COUT), bf16),
            pltpu.VMEM((BAGS * MSG, COUT), bf16),
            pltpu.VMEM((4 * ROWS, BAGS * MSG), bf16),
            pltpu.VMEM((SLOTS, CIN), bf16),
            pltpu.VMEM((CIN, D), bf16),
            pltpu.VMEM((3, D, WIDTH), bf16),
            pltpu.VMEM((GROUP, D), bf16),
            pltpu.VMEM((GROUPS * 8, GROUP), f32),
            pltpu.VMEM((SLOTS, WIDTH), bf16),
            pltpu.VMEM((SLOTS, WIDTH), bf16),
            pltpu.VMEM((SLOTS, WIDTH), bf16),
            dma((4,)),
            dma((3,)),
            dma((2,)),
            dma((2,)),
            dma,
            dma,
            dma((1,)),
            dma((7,)),
            dma((GROUPS, HEAD_DEVS)),
            dma((3,)),
        ],
        compiler_params=pltpu.CompilerParams(
            collective_id=0, has_side_effects=True, vmem_limit_bytes=56 << 20
        ),
        name="front",
    )(frame_counts, routes, samples, latents, conv_weight, embed_weight, qkv_weight)
    mixed = pl.pallas_call(
        bag_kernel,
        out_shape=jax.ShapeDtypeStruct((2, SLOTS, COUT), bf16),
        in_specs=[SMEM, VMEM, ANY, ANY, ANY],
        out_specs=VMEM,
        scratch_shapes=[
            pltpu.VMEM((SORTED, WIDTH), bf16),
            pltpu.VMEM((SORTED, WIDTH), bf16),
            pltpu.VMEM((SORTED, WIDTH), bf16),
            pltpu.VMEM((SORTED, WIDTH), bf16),
            dma((3,)),
        ],
        compiler_params=pltpu.CompilerParams(vmem_limit_bytes=56 << 20),
        name="bag",
    )(plan, valid, q, k, v)
    return pl.pallas_call(
        back_kernel,
        out_shape=jax.ShapeDtypeStruct((TOK, D), bf16),
        in_specs=[SMEM, VMEM, ANY],
        out_specs=ANY,
        scratch_shapes=[
            pltpu.VMEM((2, SLOTS, COUT), bf16),
            pltpu.VMEM((HEAD_DEVS * TOK, SLOTS), bf16),
            pltpu.VMEM((2, HEAD_DEVS * TOK, COUT), bf16),
            dma((2,)),
            dma((2,)),
            dma((4,)),
            dma((2,)),
            dma((2,)),
        ],
        compiler_params=pltpu.CompilerParams(
            collective_id=1, has_side_effects=True, vmem_limit_bytes=56 << 20
        ),
        name="back",
    )(frame_counts, routes, mixed)


def solution(mesh):
    placed = (
        P("bag", "head", None, None, None),
        P("bag"),
        P("bag", None),
        P("bag"),
        P(),
        P(),
        P(None, None, "head"),
    )
    return jax.shard_map(
        shards, mesh=mesh, in_specs=placed, out_specs=P(("bag", "head"), None), check_vma=False
    )
```

```python
import jax
import jax.numpy as jnp
from jax import lax
from jax.experimental import pallas as pl
from jax.experimental.pallas import tpu as pltpu
from jax.sharding import PartitionSpec as P

BAGS = 32
HEAD_DEVS = 8
CORES = 2
TOK = 128
CAP = 6
MSG = 32
ROWS = BAGS * CAP
SLOTS = HEAD_DEVS * ROWS
PER_BAG = HEAD_DEVS * CAP
FRAMES_DEV = 2
CELLS = 256
CIN = 512
COUT = 128
D = 2048
WIDTH = 256
HDIM = 64
GROUPS = 4
GROUP_CLIPS = BAGS // GROUPS
PIECE = GROUP_CLIPS * CAP
GROUP = HEAD_DEVS * PIECE
ALIGN = 128
QTILE = 384
KTILE = 384
SORTED = SLOTS + 4 * ALIGN + KTILE
epsilon = 1e-06
far_below = -1e30

MESH = pl.DeviceIdType.MESH
bf16 = jnp.bfloat16
f32 = jnp.float32
i32 = jnp.int32


def iota(shape, dim):
    return lax.broadcasted_iota(i32, shape, dim)


def dot(a, b):
    return jnp.dot(a, b, preferred_element_type=f32)


def greet(bag, head):
    barrier = pltpu.get_barrier_semaphore()

    def along_bag(step, carry):
        pl.semaphore_signal(
            barrier, inc=1, device_id=(lax.rem(bag + step, BAGS), head), device_id_type=MESH
        )
        return carry

    def along_head(step, carry):
        pl.semaphore_signal(
            barrier, inc=1, device_id=(bag, lax.rem(head + step, HEAD_DEVS)), device_id_type=MESH
        )
        return carry

    lax.fori_loop(1, HEAD_DEVS, along_head, 0)
    lax.fori_loop(1, BAGS, along_bag, 0)


def met():
    pl.semaphore_wait(pltpu.get_barrier_semaphore(), BAGS + HEAD_DEVS - 2)


def front_kernel(
    count_ref,
    routes_ref,
    samples_ref,
    latents_ref,
    conv_ref,
    embed_ref,
    qkv_ref,
    q_out,
    k_out,
    v_out,
    plan_ref,
    valid_ref,
    taps,
    frames,
    sums,
    edge_out,
    edge_in,
    grid,
    scatter,
    outbox,
    inbox,
    unpack,
    rows,
    embed,
    qkv,
    normed,
    targets,
    raw,
    sorted_rows,
    load_sem,
    tap_sem,
    halo_send,
    halo_recv,
    bag_send,
    bag_recv,
    local_sem,
    head_send,
    head_recv,
    store_sem,
):
    bag = lax.axis_index("bag")
    head = lax.axis_index("head")
    core = lax.rem(head, CORES)
    chip = lax.div(head, CORES)
    count = count_ref[0]

    loads = [
        pltpu.make_async_copy(latents_ref.at[f], frames.at[f], load_sem.at[f])
        for f in range(FRAMES_DEV)
    ]
    for load in loads:
        load.start()
    for a in (2, 0, 1):
        for be in range(9):
            pltpu.make_async_copy(
                conv_ref.at[9 * a + be], taps.at[a, :, pl.ds(be * COUT, COUT)], tap_sem.at[a]
            ).start()

    weights = [
        pltpu.make_async_copy(embed_ref, embed, load_sem.at[2]),
        pltpu.make_async_copy(qkv_ref, qkv, load_sem.at[3]),
    ]
    for load in weights:
        load.start()

    edge_in[...] = jnp.zeros_like(edge_in)
    greet(bag, head)

    def taps_here(a):
        pltpu.make_async_copy(taps.at[a], taps.at[a], tap_sem.at[a]).wait()

    def add_taps(slot, a, out):
        scale = jnp.where(head * FRAMES_DEV + slot < count, 1.0, 0.0)
        cells = (frames[slot].astype(f32) * scale).astype(bf16)
        made = dot(cells, taps[a])
        for e in range(3):
            sums[out, e] += made[:, (3 + e) * COUT : (4 + e) * COUT]
            sums[out, e, 16:CELLS] += made[: CELLS - 16, e * COUT : (e + 1) * COUT]
            sums[out, e, : CELLS - 16] += made[16:, (6 + e) * COUT : (7 + e) * COUT]

    column = lax.rem(iota((CELLS, COUT), 0), 16)

    def joined(out):
        from_left = jnp.where(column == 0, 0.0, pltpu.roll(sums[out, 0], 1, 0))
        from_right = jnp.where(column == 15, 0.0, pltpu.roll(sums[out, 2], CELLS - 1, 0))
        return sums[out, 1] + from_left + from_right

    sums[...] = jnp.zeros_like(sums)
    loads[0].wait()
    taps_here(2)
    add_taps(0, 2, 2)
    edge_out[1] = joined(2)
    loads[1].wait()
    taps_here(0)
    add_taps(1, 0, 3)
    edge_out[0] = joined(3)
    met()

    def edge(side, to):
        return pltpu.make_async_remote_copy(
            src_ref=edge_out.at[side],
            dst_ref=edge_in.at[side],
            send_sem=halo_send.at[side],
            recv_sem=halo_recv.at[side],
            device_id=(bag, to),
            device_id_type=MESH,
        )

    to_right = edge(0, lax.rem(head + 1, HEAD_DEVS))
    to_left = edge(1, lax.rem(head + HEAD_DEVS - 1, HEAD_DEVS))

    @pl.when(head < HEAD_DEVS - 1)
    def _():
        to_right.start()

    @pl.when(head > 0)
    def _():
        to_left.start()

    lane = iota((1, TOK), 1)
    bag_row = iota((BAGS, TOK), 0)
    half = (lane >= TOK // 2).astype(i32)
    lanes32 = iota((BAGS, TOK), 1)
    meta = jnp.where(lanes32 == HEAD_DEVS, samples_ref[0:1, 0:1].astype(f32), 0.0)
    for h in range(HEAD_DEVS):
        named = (routes_ref[h : h + 1, :] == bag_row) & (h * FRAMES_DEV + half < count)
        per_bag = jnp.sum(named.astype(f32), axis=1, keepdims=True)
        meta = meta + jnp.where(lanes32 == h, per_bag, 0.0)
    route = routes_ref[pl.ds(head, 1), :]
    live = head * FRAMES_DEV + half < count
    named = ((route == bag_row) & live).astype(f32)
    before = (iota((TOK, TOK), 0) < iota((TOK, TOK), 1)).astype(bf16)
    rank = jnp.sum(named * dot(named.astype(bf16), before), axis=0, keepdims=True)
    target = jnp.where(live, route * MSG + rank.astype(i32), -1000)
    out_row = iota((BAGS * MSG, TOK), 0)
    for q in range(4):
        scatter[:, q * TOK : (q + 1) * TOK] = (out_row == target + CAP * q).astype(f32).astype(bf16)

    add_taps(0, 0, 1)
    add_taps(1, 2, 0)
    taps_here(1)
    add_taps(0, 1, 0)
    add_taps(1, 1, 1)

    @pl.when(head > 0)
    def _():
        to_right.wait_recv()

    @pl.when(head < HEAD_DEVS - 1)
    def _():
        to_left.wait_recv()

    for f in range(FRAMES_DEV):
        scale = jnp.where(head * FRAMES_DEV + f < count, 1.0, 0.0)
        total = (joined(f) + edge_in[f]) * scale
        grid[f * 16 : (f + 1) * 16] = total.reshape(16, 16, COUT)
    quarters = []
    for di in range(2):
        for dj in range(2):
            quarters.extend(grid[2 * r + di, pl.ds(dj, 8, stride=2), :] for r in range(16))
    patches = jnp.concatenate(quarters, axis=0).astype(bf16)

    meta_here = (iota((BAGS * MSG, BAGS), 0) == iota((BAGS * MSG, BAGS), 1) * MSG + 4 * CAP).astype(f32)
    outbox[...] = (dot(scatter[...], patches) + dot(meta_here.astype(bf16), meta.astype(bf16))).astype(bf16)

    def message(ref, at):
        return ref.at[pl.ds(pl.multiple_of(at * MSG, MSG), MSG)]

    own = pltpu.make_async_copy(message(outbox, bag), message(inbox, bag), local_sem.at[0])
    own.start()

    def send(step, carry):
        to = lax.rem(bag + step, BAGS)
        pltpu.make_async_remote_copy(
            src_ref=message(outbox, to),
            dst_ref=message(inbox, bag),
            send_sem=bag_send,
            recv_sem=bag_recv,
            device_id=(to, head),
            device_id_type=MESH,
        ).start()
        return carry

    lax.fori_loop(1, BAGS, send, 0)

    slot = iota((ROWS, BAGS * MSG), 0)
    clip_of = lax.shift_right_logical(slot * 10923, 16)
    wanted = clip_of * MSG + (slot - clip_of * CAP)
    at_col = iota((ROWS, BAGS * MSG), 1)
    for q in range(4):
        unpack[q * ROWS : (q + 1) * ROWS] = (at_col == wanted + q * CAP).astype(f32).astype(bf16)

    own.wait()
    others = inbox.at[pl.ds(0, (BAGS - 1) * MSG)]
    pltpu.make_async_copy(others, others, bag_recv).wait()

    def chunk(of):
        return rows.at[pl.ds(pl.multiple_of(of * ROWS, ROWS), ROWS)]

    unpacked = dot(unpack[...], inbox[...]).astype(bf16)
    at = pl.ds(pl.multiple_of(head * ROWS, ROWS), ROWS)
    for q in range(4):
        rows[at, q * COUT : (q + 1) * COUT] = unpacked[q * ROWS : (q + 1) * ROWS]

    sibling = chip * CORES + 1 - core

    def push(of, to, sem):
        return pltpu.make_async_remote_copy(
            src_ref=chunk(of),
            dst_ref=chunk(of),
            send_sem=head_send.at[sem],
            recv_sem=head_recv.at[of],
            device_id=(bag, to),
            device_id_type=MESH,
        )

    def peer(step):
        return lax.rem(chip + step, 4) * CORES + core

    push(head, sibling, 0).start()
    push(head, peer(1), 1).start()
    push(head, peer(3), 3).start()

    pick = (iota((BAGS, BAGS * MSG), 1) == iota((BAGS, BAGS * MSG), 0) * MSG + 4 * CAP).astype(f32)
    told = dot(pick.astype(bf16), inbox[...])
    lane_w = iota((BAGS, COUT), 1)
    row_w = iota((BAGS, COUT), 0)
    counts = jnp.where(lane_w < HEAD_DEVS, told, 0.0)
    clip_total = jnp.sum(counts, axis=1, keepdims=True)
    sample = jnp.sum(jnp.where(lane_w == HEAD_DEVS, told, 0.0), axis=1, keepdims=True)
    lower = (iota((COUT, COUT), 0) < iota((COUT, COUT), 1)).astype(f32)
    earlier = dot(counts.astype(bf16), lower.astype(bf16))

    def turned(column_of):
        return jnp.sum(jnp.where(row_w == lane_w, column_of, 0.0), axis=0, keepdims=True)

    sample_row = turned(sample + 1.0) - 1.0
    same_before = (sample_row == sample) & (lane_w < row_w)
    first = jnp.sum(jnp.where(same_before, 1.0 * PER_BAG, 0.0), axis=1, keepdims=True)
    plan_lane = iota((1, COUT), 1)
    start = jnp.zeros((1, 1), f32)
    by_sample = jnp.zeros((1, COUT), f32)
    for s in range(4):
        first = first + jnp.where(sample == s, start, 0.0)
        size = jnp.sum(jnp.where(sample == s, 1.0 * PER_BAG, 0.0), axis=0, keepdims=True)
        by_sample = by_sample + jnp.where(plan_lane == s, start, 0.0)
        by_sample = by_sample + jnp.where(plan_lane == 8 + s, size, 0.0)
        start = start + jnp.ceil(size * (1.0 / ALIGN)) * ALIGN
    plan_row = iota((8, COUT), 0)
    plan = jnp.where(plan_row == 0, turned(first), jnp.where(plan_row == 1, by_sample, 0.0))
    plan_ref[...] = plan.astype(i32)
    key = iota((BAGS, SORTED), 1).astype(f32)
    held = (key >= first) & (key < first + clip_total)
    valid_ref[...] = jnp.sum(held.astype(f32), axis=0, keepdims=True)

    col = iota((8, GROUP), 1)
    col_head = lax.shift_right_logical(col * 1366, 16)
    in_piece = col - col_head * PIECE
    col_clip = lax.shift_right_logical(in_piece * 10923, 16)
    col_slot = (in_piece - col_clip * CAP).astype(f32)
    clip_row = iota((8, GROUP), 0)
    out_at = iota((GROUP, GROUP), 0).astype(f32)
    for g in range(GROUPS):
        group_counts = counts[g * 8 : (g + 1) * 8]
        group_earlier = earlier[g * 8 : (g + 1) * 8]
        number = jnp.zeros((8, GROUP), f32)
        base = jnp.zeros((8, GROUP), f32)
        for h in range(HEAD_DEVS):
            number = jnp.where(col_head == h, group_counts[:, h : h + 1], number)
            base = jnp.where(col_head == h, group_earlier[:, h : h + 1], base)
        place = jnp.where(col_slot < number, clip_row * 1.0 * PER_BAG + base + col_slot + 1.0, 0.0)
        target = jnp.sum(jnp.where(col_clip == clip_row, place, 0.0), axis=0, keepdims=True) - 1.0
        targets[g * 8 : g * 8 + 8] = jnp.broadcast_to(target, (8, GROUP))

    def arrived(of):
        pltpu.make_async_copy(chunk(of), chunk(of), head_recv.at[of]).wait()

    def relay_near():
        arrived(peer(1))
        arrived(peer(3))
        push(peer(1), sibling, 4).start()
        push(peer(3), sibling, 5).start()
        push(peer(3 - 2 * core), peer(1 + 2 * core), 2).start()

    def relay_far():
        arrived(peer(2))
        push(peer(2), sibling, 6).start()

    for load in weights:
        load.wait()

    def project(k, carry):
        of_chip = lax.rem(chip + k + k // 2 * (5 - 2 * k), 4)
        arrived(of_chip * CORES + 1 - core)
        for c in range(CORES):
            of = pl.ds(pl.multiple_of((of_chip * CORES + c) * ROWS, ROWS), ROWS)
            embedded = dot(rows[of], embed[...]).astype(bf16).astype(f32)
            scale = lax.rsqrt(jnp.mean(embedded * embedded, axis=-1, keepdims=True) + epsilon)
            normed[c * ROWS : (c + 1) * ROWS] = (embedded * scale).astype(bf16)
        for c in range(CORES):
            for m in range(3):
                made = dot(normed[c * ROWS : (c + 1) * ROWS], qkv[m]).astype(bf16)
                if m == 0:
                    made = (made * HDIM**-0.5).astype(bf16)
                for g in range(GROUPS):
                    at = g * GROUP + (of_chip * CORES + c) * PIECE
                    part = made[g * PIECE : (g + 1) * PIECE]
                    raw[pl.ds(pl.multiple_of(at, PIECE), PIECE), m * WIDTH : (m + 1) * WIDTH] = part

        @pl.when(k == 0)
        def _():
            relay_near()

        @pl.when(k == 1)
        def _():
            relay_far()

        return carry

    lax.fori_loop(0, GROUPS, project, 0)

    outs = (q_out, k_out, v_out)

    def order(g, carry):
        at = pl.ds(pl.multiple_of(g * GROUP, GROUP), GROUP)
        target = targets[pl.ds(pl.multiple_of(g * 8, 8), 8)][0:1]
        chosen = (out_at == target).astype(f32).astype(bf16)
        for m in range(3):
            sorted_rows[m, at] = dot(chosen, raw[at, m * WIDTH : (m + 1) * WIDTH]).astype(bf16)
            pltpu.make_async_copy(sorted_rows.at[m, at], outs[m].at[at], store_sem.at[m]).start()
        return carry

    lax.fori_loop(0, GROUPS, order, 0)

    for sem in range(7):
        pltpu.make_async_copy(chunk(0), chunk(0), head_send.at[sem]).wait()
    for m in range(3):
        pltpu.make_async_copy(sorted_rows.at[m], outs[m], store_sem.at[m]).wait()
    sent = outbox.at[pl.ds(0, (BAGS - 1) * MSG)]
    pltpu.make_async_copy(sent, sent, bag_send).wait()

    @pl.when(head < HEAD_DEVS - 1)
    def _():
        to_right.wait_send()

    @pl.when(head > 0)
    def _():
        to_left.wait_send()


def bag_kernel(plan_ref, valid_ref, q_in, k_in, v_in, out_ref, q_ref, k_ref, v_ref, o_ref, load_sem):
    moves = ((k_in, k_ref, 0), (q_in, q_ref, 1), (v_in, v_ref, 2))

    def load(c, carry):
        here = pl.ds(pl.multiple_of(c * PER_BAG, PER_BAG), PER_BAG)
        there = pl.ds(pl.multiple_of(plan_ref[0, c], 16), PER_BAG)
        for source, target, sem in moves:
            pltpu.make_async_copy(source.at[here], target.at[there], load_sem.at[sem]).start()
        return carry

    for s in range(4):
        past = pl.multiple_of(plan_ref[1, s] + plan_ref[1, 8 + s], 16)
        v_ref[pl.ds(past, KTILE)] = jnp.zeros((KTILE, WIDTH), bf16)
    lax.fori_loop(0, BAGS, load, 0)
    for source, target, sem in moves:
        pltpu.make_async_copy(source, target.at[pl.ds(0, SLOTS)], load_sem.at[sem]).wait()

    heads = WIDTH // HDIM
    head_of = lax.shift_right_logical(iota((QTILE, WIDTH), 1), 6)

    def one_sample(s, sample_carry):
        start, size = plan_ref[1, s], plan_ref[1, 8 + s]

        def queries(tile, carry):
            q0 = pl.multiple_of(start + tile * QTILE, ALIGN)
            block = q_ref[pl.ds(q0, QTILE)].astype(f32)
            spread = [jnp.where(head_of == h, block, 0.0).astype(bf16) for h in range(heads)]

            def score(step, h):
                k0 = pl.multiple_of(start + step * KTILE, ALIGN)
                scores = lax.dot_general(
                    spread[h], k_ref[pl.ds(k0, KTILE)], (((1,), (1,)), ((), ())), preferred_element_type=f32
                )
                in_sample = iota((1, KTILE), 1) + step * KTILE < size
                allowed = (valid_ref[:, pl.ds(k0, KTILE)] > 0.0) & in_sample
                scores = jnp.where(allowed, scores, far_below)
                return scores, v_ref[pl.ds(k0, KTILE)]

            steps = lax.div(size + KTILE - 1, KTILE)

            def first(h):
                scores, values = score(0, h)
                top = jnp.max(scores, axis=-1, keepdims=True)
                shifted = jnp.exp(scores - top)
                norm = jnp.sum(shifted, axis=-1, keepdims=True)
                return top, norm, dot(shifted.astype(bf16), values)

            def keys(step, states):
                out = []
                for h in range(heads):
                    top, norm, total = states[h]
                    scores, values = score(step, h)
                    higher = jnp.maximum(top, jnp.max(scores, axis=-1, keepdims=True))
                    shifted = jnp.exp(scores - higher)
                    fade = jnp.exp(top - higher)
                    norm = norm * fade + jnp.sum(shifted, axis=-1, keepdims=True)
                    total = total * fade + dot(shifted.astype(bf16), values)
                    out.append((higher, norm, total))
                return tuple(out)

            def finish(states):
                mixed = jnp.zeros((QTILE, WIDTH), f32)
                for h in range(heads):
                    top, norm, total = states[h]
                    mixed = jnp.where(head_of == h, total * (1.0 / norm), mixed)
                o_ref[pl.ds(q0, QTILE)] = mixed.astype(bf16)

            @pl.when(steps == 1)
            def _():
                mixed = jnp.zeros((QTILE, WIDTH), f32)
                for h in range(heads):
                    top, norm, total = first(h)
                    mixed = jnp.where(head_of == h, total * (1.0 / norm), mixed)
                o_ref[pl.ds(q0, QTILE)] = mixed.astype(bf16)

            @pl.when(steps > 1)
            def _():
                finish(lax.fori_loop(1, steps, keys, tuple(first(h) for h in range(heads))))

            return carry

        lax.fori_loop(0, lax.div(size + QTILE - 1, QTILE), queries, 0)
        return sample_carry

    lax.fori_loop(0, 4, one_sample, 0)

    for c in range(BAGS):
        there = pl.ds(pl.multiple_of(plan_ref[0, c], 16), PER_BAG)
        for half in range(2):
            out_ref[half, c * PER_BAG : (c + 1) * PER_BAG] = o_ref[there, half * COUT : (half + 1) * COUT]


def back_kernel(
    count_ref,
    routes_ref,
    mixed_ref,
    out_ref,
    inbox,
    gather,
    home,
    bag_send,
    bag_recv,
    local_sem,
    head_send,
    head_recv,
):
    bag = lax.axis_index("bag")
    head = lax.axis_index("head")
    count = count_ref[0]
    greet(bag, head)
    met()

    def message(ref, half, at):
        return ref.at[half, pl.ds(pl.multiple_of(at * PER_BAG, PER_BAG), PER_BAG)]

    owns = []
    for half in range(2):

        def send(step, carry, half=half):
            to = lax.rem(bag + step, BAGS)
            pltpu.make_async_remote_copy(
                src_ref=message(mixed_ref, half, to),
                dst_ref=message(inbox, half, bag),
                send_sem=bag_send.at[half],
                recv_sem=bag_recv.at[half],
                device_id=(to, head),
                device_id_type=MESH,
            ).start()
            return carry

        lax.fori_loop(1, BAGS, send, 0)
        own = pltpu.make_async_copy(message(mixed_ref, half, bag), message(inbox, half, bag), local_sem.at[half])
        own.start()
        owns.append(own)

    routes_col = jnp.transpose(routes_ref[...])
    half = (iota((TOK, 1), 0) >= TOK // 2).astype(i32)
    before = (iota((TOK, TOK), 1) < iota((TOK, TOK), 0)).astype(bf16)
    at_col = iota((TOK, SLOTS), 1)
    earlier = jnp.zeros((1, TOK), f32)
    for h in range(HEAD_DEVS):
        route = routes_col[:, h : h + 1]
        live = h * FRAMES_DEV + half < count
        named = ((route == iota((TOK, TOK), 1)) & live).astype(f32)
        rank = jnp.sum(named * (dot(before, named.astype(bf16)) + earlier), axis=1, keepdims=True)
        earlier = earlier + jnp.sum(named, axis=0, keepdims=True)
        target = jnp.where(live, route * PER_BAG + rank.astype(i32), -1)
        gather[h * TOK : (h + 1) * TOK] = (at_col == target).astype(f32).astype(bf16)

    def rest(ref, half):
        return ref.at[half, pl.ds(0, (BAGS - 1) * PER_BAG)]

    def columns(half):
        return pl.ds(pl.multiple_of(head * WIDTH + half * COUT, COUT), COUT)

    keeps = []
    for half in range(2):
        owns[half].wait()
        pltpu.make_async_copy(rest(inbox, half), rest(inbox, half), bag_recv.at[half]).wait()

        def deliver(step, carry, half=half):
            to = lax.rem(head + step, HEAD_DEVS)
            at = pl.ds(pl.multiple_of(to * TOK, TOK), TOK)
            home[half, at] = dot(gather[at], inbox[half]).astype(bf16)
            pltpu.make_async_remote_copy(
                src_ref=home.at[half, at],
                dst_ref=out_ref.at[:, columns(half)],
                send_sem=head_send.at[half],
                recv_sem=head_recv.at[half],
                device_id=(bag, to),
                device_id_type=MESH,
            ).start()
            return carry

        lax.fori_loop(1, HEAD_DEVS, deliver, 0)
        at = pl.ds(pl.multiple_of(head * TOK, TOK), TOK)
        home[half, at] = dot(gather[at], inbox[half]).astype(bf16)
        keep = pltpu.make_async_copy(home.at[half, at], out_ref.at[:, columns(half)], local_sem.at[2 + half])
        keep.start()
        keeps.append(keep)
    for half in range(2):
        keeps[half].wait()
        arrived = out_ref.at[:, pl.ds(0, (HEAD_DEVS - 1) * COUT)]
        pltpu.make_async_copy(arrived, arrived, head_recv.at[half]).wait()
        left = home.at[half, pl.ds(0, (HEAD_DEVS - 1) * TOK)]
        pltpu.make_async_copy(left, left, head_send.at[half]).wait()
        pltpu.make_async_copy(rest(mixed_ref, half), rest(mixed_ref, half), bag_send.at[half]).wait()


SMEM = pl.BlockSpec(memory_space=pltpu.SMEM)
VMEM = pl.BlockSpec(memory_space=pltpu.VMEM)
ANY = pl.BlockSpec(memory_space=pl.ANY)


def shards(latents, frame_counts, routes, samples, conv_weight, embed_weight, qkv_weight):
    routes = routes.reshape(HEAD_DEVS, TOK)
    samples = samples.reshape(HEAD_DEVS, TOK)
    latents = latents.reshape(FRAMES_DEV, CELLS, CIN)
    dma = pltpu.SemaphoreType.DMA
    slot_array = jax.ShapeDtypeStruct((SLOTS, WIDTH), bf16)
    q, k, v, plan, valid = pl.pallas_call(
        front_kernel,
        out_shape=(
            slot_array,
            slot_array,
            slot_array,
            jax.ShapeDtypeStruct((8, COUT), i32),
            jax.ShapeDtypeStruct((1, SORTED), f32),
        ),
        in_specs=[SMEM, VMEM, VMEM, ANY, ANY, ANY, ANY],
        out_specs=(ANY, ANY, ANY, VMEM, VMEM),
        scratch_shapes=[
            pltpu.VMEM((3, CIN, 9 * COUT), bf16),
            pltpu.VMEM((FRAMES_DEV, CELLS, CIN), bf16),
            pltpu.VMEM((FRAMES_DEV + 2, 3, CELLS, COUT), f32),
            pltpu.VMEM((2, CELLS, COUT), f32),
            pltpu.VMEM((2, CELLS, COUT), f32),
            pltpu.VMEM((FRAMES_DEV * 16, 16, COUT), f32),
            pltpu.VMEM((BAGS * MSG, 4 * TOK), bf16),
            pltpu.VMEM((BAGS * MSG, COUT), bf16),
            pltpu.VMEM((BAGS * MSG, COUT), bf16),
            pltpu.VMEM((4 * ROWS, BAGS * MSG), bf16),
            pltpu.VMEM((SLOTS, CIN), bf16),
            pltpu.VMEM((CIN, D), bf16),
            pltpu.VMEM((3, D, WIDTH), bf16),
            pltpu.VMEM((GROUP, D), bf16),
            pltpu.VMEM((GROUPS * 8, GROUP), f32),
            pltpu.VMEM((SLOTS, 3 * WIDTH), bf16),
            pltpu.VMEM((3, SLOTS, WIDTH), bf16),
            dma((4,)),
            dma((3,)),
            dma((2,)),
            dma((2,)),
            dma,
            dma,
            dma((1,)),
            dma((7,)),
            dma((HEAD_DEVS,)),
            dma((3,)),
        ],
        compiler_params=pltpu.CompilerParams(
            collective_id=0, has_side_effects=True, vmem_limit_bytes=56 << 20
        ),
        name="front",
    )(frame_counts, routes, samples, latents, conv_weight, embed_weight, qkv_weight)
    mixed = pl.pallas_call(
        bag_kernel,
        out_shape=jax.ShapeDtypeStruct((2, SLOTS, COUT), bf16),
        in_specs=[SMEM, VMEM, ANY, ANY, ANY],
        out_specs=VMEM,
        scratch_shapes=[
            pltpu.VMEM((SORTED, WIDTH), bf16),
            pltpu.VMEM((SORTED, WIDTH), bf16),
            pltpu.VMEM((SORTED, WIDTH), bf16),
            pltpu.VMEM((SORTED, WIDTH), bf16),
            dma((3,)),
        ],
        compiler_params=pltpu.CompilerParams(vmem_limit_bytes=56 << 20),
        name="bag",
    )(plan, valid, q, k, v)
    return pl.pallas_call(
        back_kernel,
        out_shape=jax.ShapeDtypeStruct((TOK, D), bf16),
        in_specs=[SMEM, VMEM, ANY],
        out_specs=ANY,
        scratch_shapes=[
            pltpu.VMEM((2, SLOTS, COUT), bf16),
            pltpu.VMEM((HEAD_DEVS * TOK, SLOTS), bf16),
            pltpu.VMEM((2, HEAD_DEVS * TOK, COUT), bf16),
            dma((2,)),
            dma((2,)),
            dma((4,)),
            dma((2,)),
            dma((2,)),
        ],
        compiler_params=pltpu.CompilerParams(
            collective_id=1, has_side_effects=True, vmem_limit_bytes=56 << 20
        ),
        name="back",
    )(frame_counts, routes, mixed)


def solution(mesh):
    placed = (
        P("bag", "head", None, None, None),
        P("bag"),
        P("bag", None),
        P("bag"),
        P(),
        P(),
        P(None, None, "head"),
    )
    return jax.shard_map(
        shards, mesh=mesh, in_specs=placed, out_specs=P(("bag", "head"), None), check_vma=False
    )
```

```python
import jax
import jax.numpy as jnp
from jax import lax
from jax.experimental import pallas as pl
from jax.experimental.pallas import tpu as pltpu
from jax.sharding import PartitionSpec as P

BAGS = 32
HEAD_DEVS = 8
CORES = 2
TOK = 128
CAP = 6
MSG = 32
ROWS = BAGS * CAP
SLOTS = HEAD_DEVS * ROWS
PER_BAG = HEAD_DEVS * CAP
FRAMES_DEV = 2
CELLS = 256
CIN = 512
COUT = 128
D = 2048
WIDTH = 256
HDIM = 64
GROUPS = 4
GROUP_CLIPS = BAGS // GROUPS
PIECE = GROUP_CLIPS * CAP
GROUP = HEAD_DEVS * PIECE
ALIGN = 128
QTILE = 384
KTILE = 384
SORTED = SLOTS + 4 * ALIGN + KTILE
epsilon = 1e-06
far_below = -1e30

MESH = pl.DeviceIdType.MESH
bf16 = jnp.bfloat16
f32 = jnp.float32
i32 = jnp.int32


def iota(shape, dim):
    return lax.broadcasted_iota(i32, shape, dim)


def dot(a, b):
    return jnp.dot(a, b, preferred_element_type=f32)


def greet(bag, head):
    barrier = pltpu.get_barrier_semaphore()

    def along_bag(step, carry):
        pl.semaphore_signal(
            barrier, inc=1, device_id=(lax.rem(bag + step, BAGS), head), device_id_type=MESH
        )
        return carry

    def along_head(step, carry):
        pl.semaphore_signal(
            barrier, inc=1, device_id=(bag, lax.rem(head + step, HEAD_DEVS)), device_id_type=MESH
        )
        return carry

    lax.fori_loop(1, HEAD_DEVS, along_head, 0)
    lax.fori_loop(1, BAGS, along_bag, 0)


def met():
    pl.semaphore_wait(pltpu.get_barrier_semaphore(), BAGS + HEAD_DEVS - 2)


def front_kernel(
    count_ref,
    routes_ref,
    samples_ref,
    latents_ref,
    conv_ref,
    embed_ref,
    qkv_ref,
    q_out,
    k_out,
    v_out,
    plan_ref,
    valid_ref,
    taps,
    frames,
    sums,
    edge_out,
    edge_in,
    grid,
    scatter,
    outbox,
    inbox,
    unpack,
    rows,
    embed,
    qkv,
    normed,
    targets,
    raw,
    sorted_rows,
    load_sem,
    tap_sem,
    halo_send,
    halo_recv,
    bag_send,
    bag_recv,
    local_sem,
    head_send,
    head_recv,
    store_sem,
):
    bag = lax.axis_index("bag")
    head = lax.axis_index("head")
    core = lax.rem(head, CORES)
    chip = lax.div(head, CORES)
    count = count_ref[0]

    loads = [
        pltpu.make_async_copy(latents_ref.at[f], frames.at[f], load_sem.at[f])
        for f in range(FRAMES_DEV)
    ]
    for load in loads:
        load.start()
    for a in (2, 0, 1):
        for be in range(9):
            pltpu.make_async_copy(
                conv_ref.at[9 * a + be], taps.at[a, :, pl.ds(be * COUT, COUT)], tap_sem.at[a]
            ).start()

    weights = [
        pltpu.make_async_copy(embed_ref, embed, load_sem.at[2]),
        pltpu.make_async_copy(qkv_ref, qkv, load_sem.at[3]),
    ]
    edge_in[...] = jnp.zeros_like(edge_in)
    greet(bag, head)

    def taps_here(a):
        pltpu.make_async_copy(taps.at[a], taps.at[a], tap_sem.at[a]).wait()

    def add_taps(slot, a, out):
        scale = jnp.where(head * FRAMES_DEV + slot < count, 1.0, 0.0)
        cells = (frames[slot].astype(f32) * scale).astype(bf16)
        made = dot(cells, taps[a])
        for e in range(3):
            sums[out, e] += made[:, (3 + e) * COUT : (4 + e) * COUT]
            sums[out, e, 16:CELLS] += made[: CELLS - 16, e * COUT : (e + 1) * COUT]
            sums[out, e, : CELLS - 16] += made[16:, (6 + e) * COUT : (7 + e) * COUT]

    column = lax.rem(iota((CELLS, COUT), 0), 16)

    def joined(out):
        from_left = jnp.where(column == 0, 0.0, pltpu.roll(sums[out, 0], 1, 0))
        from_right = jnp.where(column == 15, 0.0, pltpu.roll(sums[out, 2], CELLS - 1, 0))
        return sums[out, 1] + from_left + from_right

    lane = iota((1, TOK), 1)
    bag_row = iota((BAGS, TOK), 0)
    half = (lane >= TOK // 2).astype(i32)
    lanes32 = iota((BAGS, TOK), 1)
    meta = jnp.where(lanes32 == HEAD_DEVS, samples_ref[0:1, 0:1].astype(f32), 0.0)
    for h in range(HEAD_DEVS):
        named = (routes_ref[h : h + 1, :] == bag_row) & (h * FRAMES_DEV + half < count)
        per_bag = jnp.sum(named.astype(f32), axis=1, keepdims=True)
        meta = meta + jnp.where(lanes32 == h, per_bag, 0.0)
    route = routes_ref[pl.ds(head, 1), :]
    live = head * FRAMES_DEV + half < count
    named = ((route == bag_row) & live).astype(f32)
    before = (iota((TOK, TOK), 0) < iota((TOK, TOK), 1)).astype(bf16)
    rank = jnp.sum(named * dot(named.astype(bf16), before), axis=0, keepdims=True)
    target = jnp.where(live, route * MSG + rank.astype(i32), -1000)
    out_row = iota((BAGS * MSG, TOK), 0)
    for q in range(4):
        scatter[:, q * TOK : (q + 1) * TOK] = (out_row == target + CAP * q).astype(f32).astype(bf16)

    sums[...] = jnp.zeros_like(sums)
    loads[0].wait()
    taps_here(2)
    add_taps(0, 2, 2)
    edge_out[1] = joined(2)
    loads[1].wait()
    taps_here(0)
    add_taps(1, 0, 3)
    edge_out[0] = joined(3)
    met()

    def edge(side, to):
        return pltpu.make_async_remote_copy(
            src_ref=edge_out.at[side],
            dst_ref=edge_in.at[side],
            send_sem=halo_send.at[side],
            recv_sem=halo_recv.at[side],
            device_id=(bag, to),
            device_id_type=MESH,
        )

    to_right = edge(0, lax.rem(head + 1, HEAD_DEVS))
    to_left = edge(1, lax.rem(head + HEAD_DEVS - 1, HEAD_DEVS))

    @pl.when(head < HEAD_DEVS - 1)
    def _():
        to_right.start()

    @pl.when(head > 0)
    def _():
        to_left.start()

    add_taps(0, 0, 1)
    add_taps(1, 2, 0)
    taps_here(1)
    for load in weights:
        load.start()
    add_taps(0, 1, 0)
    add_taps(1, 1, 1)

    @pl.when(head > 0)
    def _():
        to_right.wait_recv()

    @pl.when(head < HEAD_DEVS - 1)
    def _():
        to_left.wait_recv()

    for f in range(FRAMES_DEV):
        scale = jnp.where(head * FRAMES_DEV + f < count, 1.0, 0.0)
        total = (joined(f) + edge_in[f]) * scale
        grid[f * 16 : (f + 1) * 16] = total.reshape(16, 16, COUT)
    quarters = []
    for di in range(2):
        for dj in range(2):
            quarters.extend(grid[2 * r + di, pl.ds(dj, 8, stride=2), :] for r in range(16))
    patches = jnp.concatenate(quarters, axis=0).astype(bf16)

    meta_here = (iota((BAGS * MSG, BAGS), 0) == iota((BAGS * MSG, BAGS), 1) * MSG + 4 * CAP).astype(f32)
    outbox[...] = (dot(scatter[...], patches) + dot(meta_here.astype(bf16), meta.astype(bf16))).astype(bf16)

    def message(ref, at):
        return ref.at[pl.ds(pl.multiple_of(at * MSG, MSG), MSG)]

    own = pltpu.make_async_copy(message(outbox, bag), message(inbox, bag), local_sem.at[0])
    own.start()

    def send(step, carry):
        to = lax.rem(bag + step, BAGS)
        pltpu.make_async_remote_copy(
            src_ref=message(outbox, to),
            dst_ref=message(inbox, bag),
            send_sem=bag_send,
            recv_sem=bag_recv,
            device_id=(to, head),
            device_id_type=MESH,
        ).start()
        return carry

    lax.fori_loop(1, BAGS, send, 0)

    slot = iota((ROWS, BAGS * MSG), 0)
    clip_of = lax.shift_right_logical(slot * 10923, 16)
    wanted = clip_of * MSG + (slot - clip_of * CAP)
    at_col = iota((ROWS, BAGS * MSG), 1)
    for q in range(4):
        unpack[q * ROWS : (q + 1) * ROWS] = (at_col == wanted + q * CAP).astype(f32).astype(bf16)

    own.wait()
    others = inbox.at[pl.ds(0, (BAGS - 1) * MSG)]
    pltpu.make_async_copy(others, others, bag_recv).wait()

    def chunk(of):
        return rows.at[pl.ds(pl.multiple_of(of * ROWS, ROWS), ROWS)]

    unpacked = dot(unpack[...], inbox[...]).astype(bf16)
    at = pl.ds(pl.multiple_of(head * ROWS, ROWS), ROWS)
    for q in range(4):
        rows[at, q * COUT : (q + 1) * COUT] = unpacked[q * ROWS : (q + 1) * ROWS]

    sibling = chip * CORES + 1 - core

    def push(of, to, sem):
        return pltpu.make_async_remote_copy(
            src_ref=chunk(of),
            dst_ref=chunk(of),
            send_sem=head_send.at[sem],
            recv_sem=head_recv.at[of],
            device_id=(bag, to),
            device_id_type=MESH,
        )

    def peer(step):
        return lax.rem(chip + step, 4) * CORES + core

    push(head, sibling, 0).start()
    push(head, peer(1), 1).start()
    push(head, peer(3), 3).start()

    pick = (iota((BAGS, BAGS * MSG), 1) == iota((BAGS, BAGS * MSG), 0) * MSG + 4 * CAP).astype(f32)
    told = dot(pick.astype(bf16), inbox[...])
    lane_w = iota((BAGS, COUT), 1)
    row_w = iota((BAGS, COUT), 0)
    counts = jnp.where(lane_w < HEAD_DEVS, told, 0.0)
    clip_total = jnp.sum(counts, axis=1, keepdims=True)
    sample = jnp.sum(jnp.where(lane_w == HEAD_DEVS, told, 0.0), axis=1, keepdims=True)
    lower = (iota((COUT, COUT), 0) < iota((COUT, COUT), 1)).astype(f32)
    earlier = dot(counts.astype(bf16), lower.astype(bf16))

    def turned(column_of):
        return jnp.sum(jnp.where(row_w == lane_w, column_of, 0.0), axis=0, keepdims=True)

    sample_row = turned(sample + 1.0) - 1.0
    same_before = (sample_row == sample) & (lane_w < row_w)
    first = jnp.sum(jnp.where(same_before, 1.0 * PER_BAG, 0.0), axis=1, keepdims=True)
    plan_lane = iota((1, COUT), 1)
    start = jnp.zeros((1, 1), f32)
    by_sample = jnp.zeros((1, COUT), f32)
    for s in range(4):
        first = first + jnp.where(sample == s, start, 0.0)
        size = jnp.sum(jnp.where(sample == s, 1.0 * PER_BAG, 0.0), axis=0, keepdims=True)
        by_sample = by_sample + jnp.where(plan_lane == s, start, 0.0)
        by_sample = by_sample + jnp.where(plan_lane == 8 + s, size, 0.0)
        start = start + jnp.ceil(size * (1.0 / ALIGN)) * ALIGN
    plan_row = iota((8, COUT), 0)
    plan = jnp.where(plan_row == 0, turned(first), jnp.where(plan_row == 1, by_sample, 0.0))
    plan_ref[...] = plan.astype(i32)
    key = iota((BAGS, SORTED), 1).astype(f32)
    held = (key >= first) & (key < first + clip_total)
    valid_ref[...] = jnp.sum(held.astype(f32), axis=0, keepdims=True)

    col = iota((8, GROUP), 1)
    col_head = lax.shift_right_logical(col * 1366, 16)
    in_piece = col - col_head * PIECE
    col_clip = lax.shift_right_logical(in_piece * 10923, 16)
    col_slot = (in_piece - col_clip * CAP).astype(f32)
    clip_row = iota((8, GROUP), 0)
    out_at = iota((GROUP, GROUP), 0).astype(f32)
    for g in range(GROUPS):
        group_counts = counts[g * 8 : (g + 1) * 8]
        group_earlier = earlier[g * 8 : (g + 1) * 8]
        number = jnp.zeros((8, GROUP), f32)
        base = jnp.zeros((8, GROUP), f32)
        for h in range(HEAD_DEVS):
            number = jnp.where(col_head == h, group_counts[:, h : h + 1], number)
            base = jnp.where(col_head == h, group_earlier[:, h : h + 1], base)
        place = jnp.where(col_slot < number, clip_row * 1.0 * PER_BAG + base + col_slot + 1.0, 0.0)
        target = jnp.sum(jnp.where(col_clip == clip_row, place, 0.0), axis=0, keepdims=True) - 1.0
        targets[g * 8 : g * 8 + 8] = jnp.broadcast_to(target, (8, GROUP))

    def arrived(of):
        pltpu.make_async_copy(chunk(of), chunk(of), head_recv.at[of]).wait()

    def relay_near():
        arrived(peer(1))
        arrived(peer(3))
        push(peer(1), sibling, 4).start()
        push(peer(3), sibling, 5).start()
        push(peer(3 - 2 * core), peer(1 + 2 * core), 2).start()

    def relay_far():
        arrived(peer(2))
        push(peer(2), sibling, 6).start()

    for load in weights:
        load.wait()

    def project(k, carry):
        of_chip = lax.rem(chip + k + k // 2 * (5 - 2 * k), 4)
        arrived(of_chip * CORES + 1 - core)
        for c in range(CORES):
            of = pl.ds(pl.multiple_of((of_chip * CORES + c) * ROWS, ROWS), ROWS)
            embedded = dot(rows[of], embed[...]).astype(bf16).astype(f32)
            scale = lax.rsqrt(jnp.mean(embedded * embedded, axis=-1, keepdims=True) + epsilon)
            normed[c * ROWS : (c + 1) * ROWS] = (embedded * scale).astype(bf16)
        for c in range(CORES):
            for m in range(3):
                made = dot(normed[c * ROWS : (c + 1) * ROWS], qkv[m]).astype(bf16)
                if m == 0:
                    made = (made * HDIM**-0.5).astype(bf16)
                for g in range(GROUPS):
                    at = g * GROUP + (of_chip * CORES + c) * PIECE
                    part = made[g * PIECE : (g + 1) * PIECE]
                    raw[pl.ds(pl.multiple_of(at, PIECE), PIECE), m * WIDTH : (m + 1) * WIDTH] = part

        @pl.when(k == 0)
        def _():
            relay_near()

        @pl.when(k == 1)
        def _():
            relay_far()

        return carry

    lax.fori_loop(0, GROUPS, project, 0)

    outs = (q_out, k_out, v_out)

    def order(g, carry):
        at = pl.ds(pl.multiple_of(g * GROUP, GROUP), GROUP)
        target = targets[pl.ds(pl.multiple_of(g * 8, 8), 8)][0:1]
        chosen = (out_at == target).astype(f32).astype(bf16)
        for m in range(3):
            sorted_rows[m, at] = dot(chosen, raw[at, m * WIDTH : (m + 1) * WIDTH]).astype(bf16)
            pltpu.make_async_copy(sorted_rows.at[m, at], outs[m].at[at], store_sem.at[m]).start()
        return carry

    lax.fori_loop(0, GROUPS, order, 0)

    for sem in range(7):
        pltpu.make_async_copy(chunk(0), chunk(0), head_send.at[sem]).wait()
    for m in range(3):
        pltpu.make_async_copy(sorted_rows.at[m], outs[m], store_sem.at[m]).wait()
    sent = outbox.at[pl.ds(0, (BAGS - 1) * MSG)]
    pltpu.make_async_copy(sent, sent, bag_send).wait()

    @pl.when(head < HEAD_DEVS - 1)
    def _():
        to_right.wait_send()

    @pl.when(head > 0)
    def _():
        to_left.wait_send()


def bag_kernel(plan_ref, valid_ref, q_in, k_in, v_in, out_ref, q_ref, k_ref, v_ref, o_ref, load_sem):
    moves = ((k_in, k_ref, 0), (q_in, q_ref, 1), (v_in, v_ref, 2))

    def load(c, carry):
        here = pl.ds(pl.multiple_of(c * PER_BAG, PER_BAG), PER_BAG)
        there = pl.ds(pl.multiple_of(plan_ref[0, c], 16), PER_BAG)
        for source, target, sem in moves:
            pltpu.make_async_copy(source.at[here], target.at[there], load_sem.at[sem]).start()
        return carry

    for s in range(4):
        past = pl.multiple_of(plan_ref[1, s] + plan_ref[1, 8 + s], 16)
        v_ref[pl.ds(past, KTILE)] = jnp.zeros((KTILE, WIDTH), bf16)
    lax.fori_loop(0, BAGS, load, 0)
    for source, target, sem in moves:
        pltpu.make_async_copy(source, target.at[pl.ds(0, SLOTS)], load_sem.at[sem]).wait()

    heads = WIDTH // HDIM
    head_of = lax.shift_right_logical(iota((QTILE, WIDTH), 1), 6)

    def one_sample(s, sample_carry):
        start, size = plan_ref[1, s], plan_ref[1, 8 + s]

        def queries(tile, carry):
            q0 = pl.multiple_of(start + tile * QTILE, ALIGN)
            block = q_ref[pl.ds(q0, QTILE)].astype(f32)
            spread = [jnp.where(head_of == h, block, 0.0).astype(bf16) for h in range(heads)]

            def score(step, h):
                k0 = pl.multiple_of(start + step * KTILE, ALIGN)
                scores = lax.dot_general(
                    spread[h], k_ref[pl.ds(k0, KTILE)], (((1,), (1,)), ((), ())), preferred_element_type=f32
                )
                in_sample = iota((1, KTILE), 1) + step * KTILE < size
                allowed = (valid_ref[:, pl.ds(k0, KTILE)] > 0.0) & in_sample
                scores = jnp.where(allowed, scores, far_below)
                return scores, v_ref[pl.ds(k0, KTILE)]

            steps = lax.div(size + KTILE - 1, KTILE)

            def first(h):
                scores, values = score(0, h)
                top = jnp.max(scores, axis=-1, keepdims=True)
                shifted = jnp.exp(scores - top)
                norm = jnp.sum(shifted, axis=-1, keepdims=True)
                return top, norm, dot(shifted.astype(bf16), values)

            def keys(step, states):
                out = []
                for h in range(heads):
                    top, norm, total = states[h]
                    scores, values = score(step, h)
                    higher = jnp.maximum(top, jnp.max(scores, axis=-1, keepdims=True))
                    shifted = jnp.exp(scores - higher)
                    fade = jnp.exp(top - higher)
                    norm = norm * fade + jnp.sum(shifted, axis=-1, keepdims=True)
                    total = total * fade + dot(shifted.astype(bf16), values)
                    out.append((higher, norm, total))
                return tuple(out)

            def finish(states):
                mixed = jnp.zeros((QTILE, WIDTH), f32)
                for h in range(heads):
                    top, norm, total = states[h]
                    mixed = jnp.where(head_of == h, total * (1.0 / norm), mixed)
                o_ref[pl.ds(q0, QTILE)] = mixed.astype(bf16)

            @pl.when(steps == 1)
            def _():
                mixed = jnp.zeros((QTILE, WIDTH), f32)
                for h in range(heads):
                    top, norm, total = first(h)
                    mixed = jnp.where(head_of == h, total * (1.0 / norm), mixed)
                o_ref[pl.ds(q0, QTILE)] = mixed.astype(bf16)

            @pl.when(steps > 1)
            def _():
                finish(lax.fori_loop(1, steps, keys, tuple(first(h) for h in range(heads))))

            return carry

        lax.fori_loop(0, lax.div(size + QTILE - 1, QTILE), queries, 0)
        return sample_carry

    lax.fori_loop(0, 4, one_sample, 0)

    for c in range(BAGS):
        there = pl.ds(pl.multiple_of(plan_ref[0, c], 16), PER_BAG)
        for half in range(2):
            out_ref[half, c * PER_BAG : (c + 1) * PER_BAG] = o_ref[there, half * COUT : (half + 1) * COUT]


def back_kernel(
    count_ref,
    routes_ref,
    mixed_ref,
    out_ref,
    inbox,
    gather,
    home,
    bag_send,
    bag_recv,
    local_sem,
    head_send,
    head_recv,
):
    bag = lax.axis_index("bag")
    head = lax.axis_index("head")
    count = count_ref[0]
    greet(bag, head)
    met()

    def message(ref, half, at):
        return ref.at[half, pl.ds(pl.multiple_of(at * PER_BAG, PER_BAG), PER_BAG)]

    owns = []
    for half in range(2):

        def send(step, carry, half=half):
            to = lax.rem(bag + step, BAGS)
            pltpu.make_async_remote_copy(
                src_ref=message(mixed_ref, half, to),
                dst_ref=message(inbox, half, bag),
                send_sem=bag_send.at[half],
                recv_sem=bag_recv.at[half],
                device_id=(to, head),
                device_id_type=MESH,
            ).start()
            return carry

        lax.fori_loop(1, BAGS, send, 0)
        own = pltpu.make_async_copy(message(mixed_ref, half, bag), message(inbox, half, bag), local_sem.at[half])
        own.start()
        owns.append(own)

    routes_col = jnp.transpose(routes_ref[...])
    half = (iota((TOK, 1), 0) >= TOK // 2).astype(i32)
    before = (iota((TOK, TOK), 1) < iota((TOK, TOK), 0)).astype(bf16)
    at_col = iota((TOK, SLOTS), 1)
    earlier = jnp.zeros((1, TOK), f32)
    for h in range(HEAD_DEVS):
        route = routes_col[:, h : h + 1]
        live = h * FRAMES_DEV + half < count
        named = ((route == iota((TOK, TOK), 1)) & live).astype(f32)
        rank = jnp.sum(named * (dot(before, named.astype(bf16)) + earlier), axis=1, keepdims=True)
        earlier = earlier + jnp.sum(named, axis=0, keepdims=True)
        target = jnp.where(live, route * PER_BAG + rank.astype(i32), -1)
        gather[h * TOK : (h + 1) * TOK] = (at_col == target).astype(f32).astype(bf16)

    def rest(ref, half):
        return ref.at[half, pl.ds(0, (BAGS - 1) * PER_BAG)]

    def columns(half):
        return pl.ds(pl.multiple_of(head * WIDTH + half * COUT, COUT), COUT)

    keeps = []
    for half in range(2):
        owns[half].wait()
        pltpu.make_async_copy(rest(inbox, half), rest(inbox, half), bag_recv.at[half]).wait()

        def deliver(step, carry, half=half):
            to = lax.rem(head + step, HEAD_DEVS)
            at = pl.ds(pl.multiple_of(to * TOK, TOK), TOK)
            home[half, at] = dot(gather[at], inbox[half]).astype(bf16)
            pltpu.make_async_remote_copy(
                src_ref=home.at[half, at],
                dst_ref=out_ref.at[:, columns(half)],
                send_sem=head_send.at[half],
                recv_sem=head_recv.at[half],
                device_id=(bag, to),
                device_id_type=MESH,
            ).start()
            return carry

        lax.fori_loop(1, HEAD_DEVS, deliver, 0)
        at = pl.ds(pl.multiple_of(head * TOK, TOK), TOK)
        home[half, at] = dot(gather[at], inbox[half]).astype(bf16)
        keep = pltpu.make_async_copy(home.at[half, at], out_ref.at[:, columns(half)], local_sem.at[2 + half])
        keep.start()
        keeps.append(keep)
    for half in range(2):
        keeps[half].wait()
        arrived = out_ref.at[:, pl.ds(0, (HEAD_DEVS - 1) * COUT)]
        pltpu.make_async_copy(arrived, arrived, head_recv.at[half]).wait()
        left = home.at[half, pl.ds(0, (HEAD_DEVS - 1) * TOK)]
        pltpu.make_async_copy(left, left, head_send.at[half]).wait()
        pltpu.make_async_copy(rest(mixed_ref, half), rest(mixed_ref, half), bag_send.at[half]).wait()


SMEM = pl.BlockSpec(memory_space=pltpu.SMEM)
VMEM = pl.BlockSpec(memory_space=pltpu.VMEM)
ANY = pl.BlockSpec(memory_space=pl.ANY)


def shards(latents, frame_counts, routes, samples, conv_weight, embed_weight, qkv_weight):
    routes = routes.reshape(HEAD_DEVS, TOK)
    samples = samples.reshape(HEAD_DEVS, TOK)
    latents = latents.reshape(FRAMES_DEV, CELLS, CIN)
    dma = pltpu.SemaphoreType.DMA
    slot_array = jax.ShapeDtypeStruct((SLOTS, WIDTH), bf16)
    q, k, v, plan, valid = pl.pallas_call(
        front_kernel,
        out_shape=(
            slot_array,
            slot_array,
            slot_array,
            jax.ShapeDtypeStruct((8, COUT), i32),
            jax.ShapeDtypeStruct((1, SORTED), f32),
        ),
        in_specs=[SMEM, VMEM, VMEM, ANY, ANY, ANY, ANY],
        out_specs=(ANY, ANY, ANY, VMEM, VMEM),
        scratch_shapes=[
            pltpu.VMEM((3, CIN, 9 * COUT), bf16),
            pltpu.VMEM((FRAMES_DEV, CELLS, CIN), bf16),
            pltpu.VMEM((FRAMES_DEV + 2, 3, CELLS, COUT), f32),
            pltpu.VMEM((2, CELLS, COUT), f32),
            pltpu.VMEM((2, CELLS, COUT), f32),
            pltpu.VMEM((FRAMES_DEV * 16, 16, COUT), f32),
            pltpu.VMEM((BAGS * MSG, 4 * TOK), bf16),
            pltpu.VMEM((BAGS * MSG, COUT), bf16),
            pltpu.VMEM((BAGS * MSG, COUT), bf16),
            pltpu.VMEM((4 * ROWS, BAGS * MSG), bf16),
            pltpu.VMEM((SLOTS, CIN), bf16),
            pltpu.VMEM((CIN, D), bf16),
            pltpu.VMEM((3, D, WIDTH), bf16),
            pltpu.VMEM((GROUP, D), bf16),
            pltpu.VMEM((GROUPS * 8, GROUP), f32),
            pltpu.VMEM((SLOTS, 3 * WIDTH), bf16),
            pltpu.VMEM((3, SLOTS, WIDTH), bf16),
            dma((4,)),
            dma((3,)),
            dma((2,)),
            dma((2,)),
            dma,
            dma,
            dma((1,)),
            dma((7,)),
            dma((HEAD_DEVS,)),
            dma((3,)),
        ],
        compiler_params=pltpu.CompilerParams(
            collective_id=0, has_side_effects=True, vmem_limit_bytes=56 << 20
        ),
        name="front",
    )(frame_counts, routes, samples, latents, conv_weight, embed_weight, qkv_weight)
    mixed = pl.pallas_call(
        bag_kernel,
        out_shape=pltpu.VMEM((2, SLOTS, COUT), bf16),
        in_specs=[SMEM, VMEM, ANY, ANY, ANY],
        out_specs=VMEM,
        scratch_shapes=[
            pltpu.VMEM((SORTED, WIDTH), bf16),
            pltpu.VMEM((SORTED, WIDTH), bf16),
            pltpu.VMEM((SORTED, WIDTH), bf16),
            pltpu.VMEM((SORTED, WIDTH), bf16),
            dma((3,)),
        ],
        compiler_params=pltpu.CompilerParams(vmem_limit_bytes=56 << 20),
        name="bag",
    )(plan, valid, q, k, v)
    return pl.pallas_call(
        back_kernel,
        out_shape=pltpu.VMEM((TOK, D), bf16),
        in_specs=[SMEM, VMEM, ANY],
        out_specs=ANY,
        scratch_shapes=[
            pltpu.VMEM((2, SLOTS, COUT), bf16),
            pltpu.VMEM((HEAD_DEVS * TOK, SLOTS), bf16),
            pltpu.VMEM((2, HEAD_DEVS * TOK, COUT), bf16),
            dma((2,)),
            dma((2,)),
            dma((4,)),
            dma((2,)),
            dma((2,)),
        ],
        compiler_params=pltpu.CompilerParams(
            collective_id=1, has_side_effects=True, vmem_limit_bytes=40 << 20
        ),
        name="back",
    )(frame_counts, routes, mixed)


def solution(mesh):
    placed = (
        P("bag", "head", None, None, None),
        P("bag"),
        P("bag", None),
        P("bag"),
        P(),
        P(),
        P(None, None, "head"),
    )
    return jax.shard_map(
        shards, mesh=mesh, in_specs=placed, out_specs=P(("bag", "head"), None), check_vma=False
    )
```

```python
import jax
import jax.numpy as jnp
from jax import lax
from jax.experimental import pallas as pl
from jax.experimental.pallas import tpu as pltpu
from jax.sharding import PartitionSpec as P

BAGS = 32
HEAD_DEVS = 8
CORES = 2
TOK = 128
CAP = 6
MSG = 32
ROWS = BAGS * CAP
SLOTS = HEAD_DEVS * ROWS
PER_BAG = HEAD_DEVS * CAP
FRAMES_DEV = 2
CELLS = 256
CIN = 512
COUT = 128
D = 2048
WIDTH = 256
HDIM = 64
GROUPS = 4
GROUP_CLIPS = BAGS // GROUPS
PIECE = GROUP_CLIPS * CAP
GROUP = HEAD_DEVS * PIECE
ALIGN = 128
QTILE = 384
KTILE = 384
SORTED = SLOTS + 4 * ALIGN + KTILE
epsilon = 1e-06
far_below = -1e30

MESH = pl.DeviceIdType.MESH
bf16 = jnp.bfloat16
f32 = jnp.float32
i32 = jnp.int32


def iota(shape, dim):
    return lax.broadcasted_iota(i32, shape, dim)


def dot(a, b):
    return jnp.dot(a, b, preferred_element_type=f32)


def greet(bag, head):
    barrier = pltpu.get_barrier_semaphore()

    def along_bag(step, carry):
        pl.semaphore_signal(
            barrier, inc=1, device_id=(lax.rem(bag + step, BAGS), head), device_id_type=MESH
        )
        return carry

    def along_head(step, carry):
        pl.semaphore_signal(
            barrier, inc=1, device_id=(bag, lax.rem(head + step, HEAD_DEVS)), device_id_type=MESH
        )
        return carry

    lax.fori_loop(1, HEAD_DEVS, along_head, 0)
    lax.fori_loop(1, BAGS, along_bag, 0)


def met():
    pl.semaphore_wait(pltpu.get_barrier_semaphore(), BAGS + HEAD_DEVS - 2)


def front_kernel(
    count_ref,
    routes_ref,
    samples_ref,
    latents_ref,
    conv_ref,
    embed_ref,
    qkv_ref,
    q_out,
    k_out,
    v_out,
    plan_ref,
    valid_ref,
    taps,
    frames,
    sums,
    edge_out,
    edge_in,
    grid,
    scatter,
    outbox,
    inbox,
    unpack,
    rows,
    embed,
    qkv,
    normed,
    targets,
    raw,
    sorted_rows,
    load_sem,
    tap_sem,
    halo_send,
    halo_recv,
    bag_send,
    bag_recv,
    local_sem,
    head_send,
    head_recv,
    store_sem,
):
    bag = lax.axis_index("bag")
    head = lax.axis_index("head")
    core = lax.rem(head, CORES)
    chip = lax.div(head, CORES)
    count = count_ref[0]

    loads = [
        pltpu.make_async_copy(latents_ref.at[f], frames.at[f], load_sem.at[f])
        for f in range(FRAMES_DEV)
    ]
    for load in loads:
        load.start()
    for a in (2, 0, 1):
        for be in range(9):
            pltpu.make_async_copy(
                conv_ref.at[9 * a + be], taps.at[a, :, pl.ds(be * COUT, COUT)], tap_sem.at[a]
            ).start()

    weights = [
        pltpu.make_async_copy(embed_ref, embed, load_sem.at[2]),
        pltpu.make_async_copy(qkv_ref, qkv, load_sem.at[3]),
    ]
    edge_in[...] = jnp.zeros_like(edge_in)
    greet(bag, head)

    def taps_here(a):
        pltpu.make_async_copy(taps.at[a], taps.at[a], tap_sem.at[a]).wait()

    def add_taps(slot, a, out):
        scale = jnp.where(head * FRAMES_DEV + slot < count, 1.0, 0.0)
        cells = (frames[slot].astype(f32) * scale).astype(bf16)
        made = dot(cells, taps[a])
        for e in range(3):
            sums[out, e] += made[:, (3 + e) * COUT : (4 + e) * COUT]
            sums[out, e, 16:CELLS] += made[: CELLS - 16, e * COUT : (e + 1) * COUT]
            sums[out, e, : CELLS - 16] += made[16:, (6 + e) * COUT : (7 + e) * COUT]

    column = lax.rem(iota((CELLS, COUT), 0), 16)

    def joined(out):
        from_left = jnp.where(column == 0, 0.0, pltpu.roll(sums[out, 0], 1, 0))
        from_right = jnp.where(column == 15, 0.0, pltpu.roll(sums[out, 2], CELLS - 1, 0))
        return sums[out, 1] + from_left + from_right

    lane = iota((1, TOK), 1)
    bag_row = iota((BAGS, TOK), 0)
    half = (lane >= TOK // 2).astype(i32)
    lanes32 = iota((BAGS, TOK), 1)
    meta = jnp.where(lanes32 == HEAD_DEVS, samples_ref[0:1, 0:1].astype(f32), 0.0)
    for h in range(HEAD_DEVS):
        named = (routes_ref[h : h + 1, :] == bag_row) & (h * FRAMES_DEV + half < count)
        per_bag = jnp.sum(named.astype(f32), axis=1, keepdims=True)
        meta = meta + jnp.where(lanes32 == h, per_bag, 0.0)
    route = routes_ref[pl.ds(head, 1), :]
    live = head * FRAMES_DEV + half < count
    named = ((route == bag_row) & live).astype(f32)
    before = (iota((TOK, TOK), 0) < iota((TOK, TOK), 1)).astype(bf16)
    rank = jnp.sum(named * dot(named.astype(bf16), before), axis=0, keepdims=True)
    target = jnp.where(live, route * MSG + rank.astype(i32), -1000)
    out_row = iota((BAGS * MSG, TOK), 0)
    for q in range(4):
        scatter[:, q * TOK : (q + 1) * TOK] = (out_row == target + CAP * q).astype(f32).astype(bf16)

    sums[...] = jnp.zeros_like(sums)
    loads[0].wait()
    taps_here(2)
    add_taps(0, 2, 2)
    edge_out[1] = joined(2)
    loads[1].wait()
    taps_here(0)
    add_taps(1, 0, 3)
    edge_out[0] = joined(3)
    met()

    def edge(side, to):
        return pltpu.make_async_remote_copy(
            src_ref=edge_out.at[side],
            dst_ref=edge_in.at[side],
            send_sem=halo_send.at[side],
            recv_sem=halo_recv.at[side],
            device_id=(bag, to),
            device_id_type=MESH,
        )

    to_right = edge(0, lax.rem(head + 1, HEAD_DEVS))
    to_left = edge(1, lax.rem(head + HEAD_DEVS - 1, HEAD_DEVS))

    @pl.when(head < HEAD_DEVS - 1)
    def _():
        to_right.start()

    @pl.when(head > 0)
    def _():
        to_left.start()

    add_taps(0, 0, 1)
    add_taps(1, 2, 0)
    taps_here(1)
    for load in weights:
        load.start()
    add_taps(0, 1, 0)
    add_taps(1, 1, 1)

    @pl.when(head > 0)
    def _():
        to_right.wait_recv()

    @pl.when(head < HEAD_DEVS - 1)
    def _():
        to_left.wait_recv()

    for f in range(FRAMES_DEV):
        scale = jnp.where(head * FRAMES_DEV + f < count, 1.0, 0.0)
        total = (joined(f) + edge_in[f]) * scale
        grid[f * 16 : (f + 1) * 16] = total.reshape(16, 16, COUT)
    quarters = []
    for di in range(2):
        for dj in range(2):
            quarters.extend(grid[2 * r + di, pl.ds(dj, 8, stride=2), :] for r in range(16))
    patches = jnp.concatenate(quarters, axis=0).astype(bf16)

    meta_here = (iota((BAGS * MSG, BAGS), 0) == iota((BAGS * MSG, BAGS), 1) * MSG + 4 * CAP).astype(f32)
    outbox[...] = (dot(scatter[...], patches) + dot(meta_here.astype(bf16), meta.astype(bf16))).astype(bf16)

    def message(ref, at):
        return ref.at[pl.ds(pl.multiple_of(at * MSG, MSG), MSG)]

    own = pltpu.make_async_copy(message(outbox, bag), message(inbox, bag), local_sem.at[0])
    own.start()

    def send(step, carry):
        to = lax.rem(bag + step, BAGS)
        pltpu.make_async_remote_copy(
            src_ref=message(outbox, to),
            dst_ref=message(inbox, bag),
            send_sem=bag_send,
            recv_sem=bag_recv,
            device_id=(to, head),
            device_id_type=MESH,
        ).start()
        return carry

    lax.fori_loop(1, BAGS, send, 0)

    slot = iota((ROWS, BAGS * MSG), 0)
    clip_of = lax.shift_right_logical(slot * 10923, 16)
    wanted = clip_of * MSG + (slot - clip_of * CAP)
    at_col = iota((ROWS, BAGS * MSG), 1)
    for q in range(4):
        unpack[q * ROWS : (q + 1) * ROWS] = (at_col == wanted + q * CAP).astype(f32).astype(bf16)

    own.wait()
    others = inbox.at[pl.ds(0, (BAGS - 1) * MSG)]
    pltpu.make_async_copy(others, others, bag_recv).wait()

    def chunk(of):
        return rows.at[pl.ds(pl.multiple_of(of * ROWS, ROWS), ROWS)]

    unpacked = dot(unpack[...], inbox[...]).astype(bf16)
    at = pl.ds(pl.multiple_of(head * ROWS, ROWS), ROWS)
    for q in range(4):
        rows[at, q * COUT : (q + 1) * COUT] = unpacked[q * ROWS : (q + 1) * ROWS]

    sibling = chip * CORES + 1 - core

    def push(of, to, sem):
        return pltpu.make_async_remote_copy(
            src_ref=chunk(of),
            dst_ref=chunk(of),
            send_sem=head_send.at[sem],
            recv_sem=head_recv.at[of],
            device_id=(bag, to),
            device_id_type=MESH,
        )

    def peer(step):
        return lax.rem(chip + step, 4) * CORES + core

    push(head, sibling, 0).start()
    push(head, peer(1), 1).start()
    push(head, peer(3), 3).start()

    pick = (iota((BAGS, BAGS * MSG), 1) == iota((BAGS, BAGS * MSG), 0) * MSG + 4 * CAP).astype(f32)
    told = dot(pick.astype(bf16), inbox[...])
    lane_w = iota((BAGS, COUT), 1)
    row_w = iota((BAGS, COUT), 0)
    counts = jnp.where(lane_w < HEAD_DEVS, told, 0.0)
    clip_total = jnp.sum(counts, axis=1, keepdims=True)
    sample = jnp.sum(jnp.where(lane_w == HEAD_DEVS, told, 0.0), axis=1, keepdims=True)
    lower = (iota((COUT, COUT), 0) < iota((COUT, COUT), 1)).astype(f32)
    earlier = dot(counts.astype(bf16), lower.astype(bf16))

    def turned(column_of):
        return jnp.sum(jnp.where(row_w == lane_w, column_of, 0.0), axis=0, keepdims=True)

    sample_row = turned(sample + 1.0) - 1.0
    same_before = (sample_row == sample) & (lane_w < row_w)
    first = jnp.sum(jnp.where(same_before, 1.0 * PER_BAG, 0.0), axis=1, keepdims=True)
    plan_lane = iota((1, COUT), 1)
    start = jnp.zeros((1, 1), f32)
    by_sample = jnp.zeros((1, COUT), f32)
    for s in range(4):
        first = first + jnp.where(sample == s, start, 0.0)
        size = jnp.sum(jnp.where(sample == s, 1.0 * PER_BAG, 0.0), axis=0, keepdims=True)
        by_sample = by_sample + jnp.where(plan_lane == s, start, 0.0)
        by_sample = by_sample + jnp.where(plan_lane == 8 + s, size, 0.0)
        start = start + jnp.ceil(size * (1.0 / ALIGN)) * ALIGN
    plan_row = iota((8, COUT), 0)
    plan = jnp.where(plan_row == 0, turned(first), jnp.where(plan_row == 1, by_sample, 0.0))
    plan_ref[...] = plan.astype(i32)
    key = iota((BAGS, SORTED), 1).astype(f32)
    held = (key >= first) & (key < first + clip_total)
    valid_ref[...] = jnp.sum(held.astype(f32), axis=0, keepdims=True)

    col = iota((8, GROUP), 1)
    col_head = lax.shift_right_logical(col * 1366, 16)
    in_piece = col - col_head * PIECE
    col_clip = lax.shift_right_logical(in_piece * 10923, 16)
    col_slot = (in_piece - col_clip * CAP).astype(f32)
    clip_row = iota((8, GROUP), 0)
    out_at = iota((GROUP, GROUP), 0).astype(f32)
    for g in range(GROUPS):
        group_counts = counts[g * 8 : (g + 1) * 8]
        group_earlier = earlier[g * 8 : (g + 1) * 8]
        number = jnp.zeros((8, GROUP), f32)
        base = jnp.zeros((8, GROUP), f32)
        for h in range(HEAD_DEVS):
            number = jnp.where(col_head == h, group_counts[:, h : h + 1], number)
            base = jnp.where(col_head == h, group_earlier[:, h : h + 1], base)
        place = jnp.where(col_slot < number, clip_row * 1.0 * PER_BAG + base + col_slot + 1.0, 0.0)
        target = jnp.sum(jnp.where(col_clip == clip_row, place, 0.0), axis=0, keepdims=True) - 1.0
        targets[g * GROUP : (g + 1) * GROUP] = (out_at == target).astype(f32).astype(bf16)

    def arrived(of):
        pltpu.make_async_copy(chunk(of), chunk(of), head_recv.at[of]).wait()

    def relay_near():
        arrived(peer(1))
        arrived(peer(3))
        push(peer(1), sibling, 4).start()
        push(peer(3), sibling, 5).start()
        push(peer(3 - 2 * core), peer(1 + 2 * core), 2).start()

    def relay_far():
        arrived(peer(2))
        push(peer(2), sibling, 6).start()

    for load in weights:
        load.wait()

    def project(k, carry):
        of_chip = lax.rem(chip + k + k // 2 * (5 - 2 * k), 4)
        arrived(of_chip * CORES + 1 - core)
        for c in range(CORES):
            of = pl.ds(pl.multiple_of((of_chip * CORES + c) * ROWS, ROWS), ROWS)
            embedded = dot(rows[of], embed[...]).astype(bf16).astype(f32)
            scale = lax.rsqrt(jnp.mean(embedded * embedded, axis=-1, keepdims=True) + epsilon)
            normed[c * ROWS : (c + 1) * ROWS] = (embedded * scale).astype(bf16)
        for c in range(CORES):
            for m in range(3):
                made = dot(normed[c * ROWS : (c + 1) * ROWS], qkv[m]).astype(bf16)
                if m == 0:
                    made = (made * HDIM**-0.5).astype(bf16)
                for g in range(GROUPS):
                    at = g * GROUP + (of_chip * CORES + c) * PIECE
                    part = made[g * PIECE : (g + 1) * PIECE]
                    raw[pl.ds(pl.multiple_of(at, PIECE), PIECE), m * WIDTH : (m + 1) * WIDTH] = part

        @pl.when(k == 0)
        def _():
            relay_near()

        @pl.when(k == 1)
        def _():
            relay_far()

        return carry

    lax.fori_loop(0, GROUPS, project, 0)

    outs = (q_out, k_out, v_out)

    def order(g, carry):
        at = pl.ds(pl.multiple_of(g * GROUP, GROUP), GROUP)
        chosen = targets[at]
        for m in range(3):
            sorted_rows[m, at] = dot(chosen, raw[at, m * WIDTH : (m + 1) * WIDTH]).astype(bf16)
            pltpu.make_async_copy(sorted_rows.at[m, at], outs[m].at[at], store_sem.at[m]).start()
        return carry

    for g in range(GROUPS):
        order(g, 0)

    for sem in range(7):
        pltpu.make_async_copy(chunk(0), chunk(0), head_send.at[sem]).wait()
    for m in range(3):
        pltpu.make_async_copy(sorted_rows.at[m], outs[m], store_sem.at[m]).wait()
    sent = outbox.at[pl.ds(0, (BAGS - 1) * MSG)]
    pltpu.make_async_copy(sent, sent, bag_send).wait()

    @pl.when(head < HEAD_DEVS - 1)
    def _():
        to_right.wait_send()

    @pl.when(head > 0)
    def _():
        to_left.wait_send()


def bag_kernel(plan_ref, valid_ref, q_in, k_in, v_in, out_ref, q_ref, k_ref, v_ref, o_ref, load_sem):
    moves = ((k_in, k_ref, 0), (q_in, q_ref, 1), (v_in, v_ref, 2))

    def load(c, carry):
        here = pl.ds(pl.multiple_of(c * PER_BAG, PER_BAG), PER_BAG)
        there = pl.ds(pl.multiple_of(plan_ref[0, c], 16), PER_BAG)
        for source, target, sem in moves:
            pltpu.make_async_copy(source.at[here], target.at[there], load_sem.at[sem]).start()
        return carry

    for s in range(4):
        past = pl.multiple_of(plan_ref[1, s] + plan_ref[1, 8 + s], 16)
        v_ref[pl.ds(past, KTILE)] = jnp.zeros((KTILE, WIDTH), bf16)
    lax.fori_loop(0, BAGS, load, 0)
    for source, target, sem in moves:
        pltpu.make_async_copy(source, target.at[pl.ds(0, SLOTS)], load_sem.at[sem]).wait()

    heads = WIDTH // HDIM
    head_of = lax.shift_right_logical(iota((QTILE, WIDTH), 1), 6)

    def one_sample(s, sample_carry):
        start, size = plan_ref[1, s], plan_ref[1, 8 + s]

        def queries(tile, carry):
            q0 = pl.multiple_of(start + tile * QTILE, ALIGN)
            block = q_ref[pl.ds(q0, QTILE)].astype(f32)
            spread = [jnp.where(head_of == h, block, 0.0).astype(bf16) for h in range(heads)]

            def score(step, h):
                k0 = pl.multiple_of(start + step * KTILE, ALIGN)
                scores = lax.dot_general(
                    spread[h], k_ref[pl.ds(k0, KTILE)], (((1,), (1,)), ((), ())), preferred_element_type=f32
                )
                in_sample = iota((1, KTILE), 1) + step * KTILE < size
                allowed = (valid_ref[:, pl.ds(k0, KTILE)] > 0.0) & in_sample
                scores = jnp.where(allowed, scores, far_below)
                return scores, v_ref[pl.ds(k0, KTILE)]

            steps = lax.div(size + KTILE - 1, KTILE)

            def first(h):
                scores, values = score(0, h)
                top = jnp.max(scores, axis=-1, keepdims=True)
                shifted = jnp.exp(scores - top)
                norm = jnp.sum(shifted, axis=-1, keepdims=True)
                return top, norm, dot(shifted.astype(bf16), values)

            def keys(step, states):
                out = []
                for h in range(heads):
                    top, norm, total = states[h]
                    scores, values = score(step, h)
                    higher = jnp.maximum(top, jnp.max(scores, axis=-1, keepdims=True))
                    shifted = jnp.exp(scores - higher)
                    fade = jnp.exp(top - higher)
                    norm = norm * fade + jnp.sum(shifted, axis=-1, keepdims=True)
                    total = total * fade + dot(shifted.astype(bf16), values)
                    out.append((higher, norm, total))
                return tuple(out)

            def finish(states):
                mixed = jnp.zeros((QTILE, WIDTH), f32)
                for h in range(heads):
                    top, norm, total = states[h]
                    mixed = jnp.where(head_of == h, total * (1.0 / norm), mixed)
                o_ref[pl.ds(q0, QTILE)] = mixed.astype(bf16)

            @pl.when(steps == 1)
            def _():
                mixed = jnp.zeros((QTILE, WIDTH), f32)
                for h in range(heads):
                    top, norm, total = first(h)
                    mixed = jnp.where(head_of == h, total * (1.0 / norm), mixed)
                o_ref[pl.ds(q0, QTILE)] = mixed.astype(bf16)

            @pl.when(steps > 1)
            def _():
                finish(lax.fori_loop(1, steps, keys, tuple(first(h) for h in range(heads))))

            return carry

        lax.fori_loop(0, lax.div(size + QTILE - 1, QTILE), queries, 0)
        return sample_carry

    lax.fori_loop(0, 4, one_sample, 0)

    for c in range(BAGS):
        there = pl.ds(pl.multiple_of(plan_ref[0, c], 16), PER_BAG)
        for half in range(2):
            out_ref[half, c * PER_BAG : (c + 1) * PER_BAG] = o_ref[there, half * COUT : (half + 1) * COUT]


def back_kernel(
    count_ref,
    routes_ref,
    mixed_ref,
    out_ref,
    inbox,
    gather,
    home,
    bag_send,
    bag_recv,
    local_sem,
    head_send,
    head_recv,
):
    bag = lax.axis_index("bag")
    head = lax.axis_index("head")
    count = count_ref[0]
    greet(bag, head)
    met()

    def message(ref, half, at):
        return ref.at[half, pl.ds(pl.multiple_of(at * PER_BAG, PER_BAG), PER_BAG)]

    owns = []
    for half in range(2):

        def send(step, carry, half=half):
            to = lax.rem(bag + step, BAGS)
            pltpu.make_async_remote_copy(
                src_ref=message(mixed_ref, half, to),
                dst_ref=message(inbox, half, bag),
                send_sem=bag_send.at[half],
                recv_sem=bag_recv.at[half],
                device_id=(to, head),
                device_id_type=MESH,
            ).start()
            return carry

        lax.fori_loop(1, BAGS, send, 0)
        own = pltpu.make_async_copy(message(mixed_ref, half, bag), message(inbox, half, bag), local_sem.at[half])
        own.start()
        owns.append(own)

    routes_col = jnp.transpose(routes_ref[...])
    half = (iota((TOK, 1), 0) >= TOK // 2).astype(i32)
    before = (iota((TOK, TOK), 1) < iota((TOK, TOK), 0)).astype(bf16)
    at_col = iota((TOK, SLOTS), 1)
    earlier = jnp.zeros((1, TOK), f32)
    for h in range(HEAD_DEVS):
        route = routes_col[:, h : h + 1]
        live = h * FRAMES_DEV + half < count
        named = ((route == iota((TOK, TOK), 1)) & live).astype(f32)
        rank = jnp.sum(named * (dot(before, named.astype(bf16)) + earlier), axis=1, keepdims=True)
        earlier = earlier + jnp.sum(named, axis=0, keepdims=True)
        target = jnp.where(live, route * PER_BAG + rank.astype(i32), -1)
        gather[h * TOK : (h + 1) * TOK] = (at_col == target).astype(f32).astype(bf16)

    def rest(ref, half):
        return ref.at[half, pl.ds(0, (BAGS - 1) * PER_BAG)]

    def columns(half):
        return pl.ds(pl.multiple_of(head * WIDTH + half * COUT, COUT), COUT)

    keeps = []
    for half in range(2):
        owns[half].wait()
        pltpu.make_async_copy(rest(inbox, half), rest(inbox, half), bag_recv.at[half]).wait()

        def deliver(step, carry, half=half):
            to = lax.rem(head + step, HEAD_DEVS)
            at = pl.ds(pl.multiple_of(to * TOK, TOK), TOK)
            home[half, at] = dot(gather[at], inbox[half]).astype(bf16)
            pltpu.make_async_remote_copy(
                src_ref=home.at[half, at],
                dst_ref=out_ref.at[:, columns(half)],
                send_sem=head_send.at[half],
                recv_sem=head_recv.at[half],
                device_id=(bag, to),
                device_id_type=MESH,
            ).start()
            return carry

        lax.fori_loop(1, HEAD_DEVS, deliver, 0)
        at = pl.ds(pl.multiple_of(head * TOK, TOK), TOK)
        home[half, at] = dot(gather[at], inbox[half]).astype(bf16)
        keep = pltpu.make_async_copy(home.at[half, at], out_ref.at[:, columns(half)], local_sem.at[2 + half])
        keep.start()
        keeps.append(keep)
    for half in range(2):
        keeps[half].wait()
        arrived = out_ref.at[:, pl.ds(0, (HEAD_DEVS - 1) * COUT)]
        pltpu.make_async_copy(arrived, arrived, head_recv.at[half]).wait()
        left = home.at[half, pl.ds(0, (HEAD_DEVS - 1) * TOK)]
        pltpu.make_async_copy(left, left, head_send.at[half]).wait()
        pltpu.make_async_copy(rest(mixed_ref, half), rest(mixed_ref, half), bag_send.at[half]).wait()


SMEM = pl.BlockSpec(memory_space=pltpu.SMEM)
VMEM = pl.BlockSpec(memory_space=pltpu.VMEM)
ANY = pl.BlockSpec(memory_space=pl.ANY)


def shards(latents, frame_counts, routes, samples, conv_weight, embed_weight, qkv_weight):
    routes = routes.reshape(HEAD_DEVS, TOK)
    samples = samples.reshape(HEAD_DEVS, TOK)
    latents = latents.reshape(FRAMES_DEV, CELLS, CIN)
    dma = pltpu.SemaphoreType.DMA
    slot_array = jax.ShapeDtypeStruct((SLOTS, WIDTH), bf16)
    q, k, v, plan, valid = pl.pallas_call(
        front_kernel,
        out_shape=(
            slot_array,
            slot_array,
            slot_array,
            jax.ShapeDtypeStruct((8, COUT), i32),
            jax.ShapeDtypeStruct((1, SORTED), f32),
        ),
        in_specs=[SMEM, VMEM, VMEM, ANY, ANY, ANY, ANY],
        out_specs=(ANY, ANY, ANY, VMEM, VMEM),
        scratch_shapes=[
            pltpu.VMEM((3, CIN, 9 * COUT), bf16),
            pltpu.VMEM((FRAMES_DEV, CELLS, CIN), bf16),
            pltpu.VMEM((FRAMES_DEV + 2, 3, CELLS, COUT), f32),
            pltpu.VMEM((2, CELLS, COUT), f32),
            pltpu.VMEM((2, CELLS, COUT), f32),
            pltpu.VMEM((FRAMES_DEV * 16, 16, COUT), f32),
            pltpu.VMEM((BAGS * MSG, 4 * TOK), bf16),
            pltpu.VMEM((BAGS * MSG, COUT), bf16),
            pltpu.VMEM((BAGS * MSG, COUT), bf16),
            pltpu.VMEM((4 * ROWS, BAGS * MSG), bf16),
            pltpu.VMEM((SLOTS, CIN), bf16),
            pltpu.VMEM((CIN, D), bf16),
            pltpu.VMEM((3, D, WIDTH), bf16),
            pltpu.VMEM((GROUP, D), bf16),
            pltpu.VMEM((GROUPS * GROUP, GROUP), bf16),
            pltpu.VMEM((SLOTS, 3 * WIDTH), bf16),
            pltpu.VMEM((3, SLOTS, WIDTH), bf16),
            dma((4,)),
            dma((3,)),
            dma((2,)),
            dma((2,)),
            dma,
            dma,
            dma((1,)),
            dma((7,)),
            dma((HEAD_DEVS,)),
            dma((3,)),
        ],
        compiler_params=pltpu.CompilerParams(
            collective_id=0, has_side_effects=True, vmem_limit_bytes=56 << 20
        ),
        name="front",
    )(frame_counts, routes, samples, latents, conv_weight, embed_weight, qkv_weight)
    mixed = pl.pallas_call(
        bag_kernel,
        out_shape=pltpu.VMEM((2, SLOTS, COUT), bf16),
        in_specs=[SMEM, VMEM, ANY, ANY, ANY],
        out_specs=VMEM,
        scratch_shapes=[
            pltpu.VMEM((SORTED, WIDTH), bf16),
            pltpu.VMEM((SORTED, WIDTH), bf16),
            pltpu.VMEM((SORTED, WIDTH), bf16),
            pltpu.VMEM((SORTED, WIDTH), bf16),
            dma((3,)),
        ],
        compiler_params=pltpu.CompilerParams(vmem_limit_bytes=56 << 20),
        name="bag",
    )(plan, valid, q, k, v)
    return pl.pallas_call(
        back_kernel,
        out_shape=pltpu.VMEM((TOK, D), bf16),
        in_specs=[SMEM, VMEM, ANY],
        out_specs=ANY,
        scratch_shapes=[
            pltpu.VMEM((2, SLOTS, COUT), bf16),
            pltpu.VMEM((HEAD_DEVS * TOK, SLOTS), bf16),
            pltpu.VMEM((2, HEAD_DEVS * TOK, COUT), bf16),
            dma((2,)),
            dma((2,)),
            dma((4,)),
            dma((2,)),
            dma((2,)),
        ],
        compiler_params=pltpu.CompilerParams(
            collective_id=1, has_side_effects=True, vmem_limit_bytes=40 << 20
        ),
        name="back",
    )(frame_counts, routes, mixed)


def solution(mesh):
    placed = (
        P("bag", "head", None, None, None),
        P("bag"),
        P("bag", None),
        P("bag"),
        P(),
        P(),
        P(None, None, "head"),
    )
    return jax.shard_map(
        shards, mesh=mesh, in_specs=placed, out_specs=P(("bag", "head"), None), check_vma=False
    )
```
